256 devices in a mesh: grp: 16 (over x, y), rank: 16 (over z, core).
Axes of the slice: x: 4, y: 4, z: 8, core: 2. Of those that a mesh axis runs over, the one named last changes fastest.
Arguments:
- queries: bfloat16 [2048, 64, 576], P(('grp', 'rank')), parts along dimension 0, may hold values from -64 to 64
- cache_pool: bfloat16 [4096, 64, 576], P(('grp', 'rank')), parts along dimension 0, may hold values from -6 to 6
- page_table: int32 [2048, 2], P(('grp', 'rank')), parts along dimension 0, may hold values from 0 to 15, as said below
- lengths: int32 [2048], P(('grp', 'rank')), parts along dimension 0, may hold values from 1 to 128, as said below
- residual: bfloat16 [2048, 3584], P(('grp', 'rank')), parts along dimension 0, may hold values from -3 to 3
- w_uv: bfloat16 [64, 512, 128], P('rank'), may hold values from -1 to 1
- w_out: bfloat16 [8192, 3584], P('rank'), may hold values from -0.125 to 0.125
- norm_gain: float32 [3584], replicated, may hold values from 0.1 to 1.9
- w_gate: bfloat16 [3584, 9216], P(None, 'rank'), may hold values from -0.09375 to 0.09375
- w_down: bfloat16 [9216, 3584], P('rank'), may hold values from -0.125 to 0.125
Outputs:
- attended: bfloat16 [2048, 3584], P(('grp', 'rank')), parts along dimension 0
- ffn_out: bfloat16 [2048, 3584], P(('grp', 'rank')), parts along dimension 0
The draws below stay inside these ranges and needn't reach their ends.
There are 16 independent parts, one for each index of `grp`. The reference program is written for one: setup_inputs(seed, part) draws one part's arguments, and reference() takes and returns one part's arrays. A program takes and returns all parts, laid end to end along the dimension named above; an argument that names none is the same for every part. Nothing has to cross between parts.
Inputs may be any that keep to these rules, and one draw needn't show every extreme that they name: `lengths`: each row's live positions lie at its start; in every group some row holds exactly 128. `page_table`: the rows of one rank use each of that rank's 16 pages exactly once.
All inputs are finite; a program needn't handle non-finite values.
Results may differ from the reference program's by a relative error of at most 0.02.
Values may be sent and summed in bfloat16 or wider, within the bound.
A program may use at most 64 MiB of HBM per device.

```python
import jax
import jax.numpy as jnp
from jax import lax

D = 3584
HEADS = 64
LAT = 512
VDIM = 128
PAGE = 64
PAGES_ROW = 2
ATT_ROWS = 8
KW = 576
CACHE = 128
PAGES_DEV = 16
POOL = 256
ROWS_ATT = 128
FF = 9216
N_RANK = 16


def pool_values(key):
    raw = jax.random.normal(jax.random.fold_in(key, 101), (POOL, PAGE, KW), jnp.float32)
    return jnp.clip(raw, -6.0, 6.0)


def page_values(key):
    rank_keys = jax.random.split(jax.random.fold_in(key, 202), N_RANK)
    page_perm = jax.vmap(lambda one_key: jax.random.permutation(one_key, PAGES_DEV))(rank_keys)
    return page_perm.reshape(ROWS_ATT, PAGES_ROW).astype(jnp.int32)


def draw_cache_pool(key, part):
    return pool_values(key).astype(jnp.bfloat16)


def draw_page_table(key, part):
    return page_values(key)


def draw_lengths(key, part):
    key = jax.random.fold_in(key, 5)
    cap_key, len_key, top_key = jax.random.split(key, 3)
    row_caps = jnp.maximum(CACHE * jax.random.randint(cap_key, (N_RANK,), 1, 9) // 8, 1)
    drawn = jax.random.randint(len_key, (N_RANK, ATT_ROWS), 0, 1048576)
    result = (1 + drawn % row_caps[:, None]).reshape(ROWS_ATT)
    longest = jax.random.randint(top_key, (), 0, ROWS_ATT)
    result = jnp.where(jnp.arange(ROWS_ATT) == longest, CACHE, result)
    return result.astype(jnp.int32)


def draw_queries(key, part):
    key = jax.random.fold_in(key, 9)
    result = 0.5 * jax.random.normal(key, (ROWS_ATT, HEADS, KW), jnp.float32)
    return result.astype(jnp.bfloat16)


def block_scale(rng, dims, cuts, low, largest):
    gain = 1.0
    for position, parts in cuts:
        steps = jax.random.uniform(jax.random.fold_in(jax.random.fold_in(rng, 6), position), (parts,), jnp.float32, low / len(cuts), largest / len(cuts))
        gain = gain * jnp.repeat(jnp.exp(steps), dims[position] // parts).reshape((-1,) + (1,) * (len(dims) - 1 - position))
    return gain


def gaussian(rng, dims, spread, reach, cuts=(), kind=jnp.bfloat16):
    level = block_scale(rng, dims, cuts, -0.22, 0.18) if cuts else 1.0
    values = jax.random.normal(rng, dims, jnp.float32) * spread * level
    return jnp.minimum(jnp.maximum(values, -reach), reach).astype(kind)


def setup_inputs(seed: int = 0, part: int = 0) -> dict:
    splits = jax.random.split(jax.random.key(seed), 11)
    own_keys = jax.random.split(jax.random.fold_in(splits[10], part), 11)
    return {
        "queries": draw_queries(jax.random.fold_in(jax.random.fold_in(splits[10], part), 71), part),
        "cache_pool": draw_cache_pool(jax.random.fold_in(jax.random.fold_in(splits[10], part), 71), part),
        "page_table": draw_page_table(jax.random.fold_in(jax.random.fold_in(splits[10], part), 71), part),
        "lengths": draw_lengths(jax.random.fold_in(jax.random.fold_in(splits[10], part), 71), part),
        "residual": gaussian(own_keys[4], (ROWS_ATT, D), 0.5, 3.0, ((0, 16),)),
        "w_uv": gaussian(splits[5], (HEADS, LAT, VDIM), (LAT // 16) ** -0.5, 1.0, ((0, 16),)),
        "w_out": gaussian(splits[6], (HEADS * VDIM, D), (HEADS * VDIM // 4) ** -0.5, 0.125, ((0, 16),)),
        "norm_gain": jnp.clip(1.0 + 0.18 * jax.random.normal(splits[7], (D,), jnp.float32), 0.1, 1.9),
        "w_gate": gaussian(splits[8], (D, FF), D ** -0.5, 0.09375, ((1, 16),)),
        "w_down": gaussian(splits[9], (FF, D), (FF // 4) ** -0.5, 0.125, ((0, 16),)),
    }


score_scale = 0.07216878364870322

def reference(queries, cache_pool, page_table, lengths, residual, w_uv, w_out, norm_gain, w_gate, w_down):
    owner_base = jnp.arange(ROWS_ATT, dtype=jnp.int32) // ATT_ROWS * PAGES_DEV
    page_index = (page_table + owner_base[:, None]).astype(jnp.int32)
    key_rows = cache_pool[page_index].reshape(ROWS_ATT, CACHE, KW)
    scores = jnp.einsum('bhk,btk->bht', queries.astype(jnp.float32), key_rows.astype(jnp.float32)) * score_scale
    is_valid = jnp.arange(CACHE, dtype=jnp.int32)[None, None, :] < lengths[:, None, None]
    scores = jnp.where(is_valid, scores, jnp.float32(-1e+30))
    weights = jax.nn.softmax(scores, axis=-1).astype(jnp.bfloat16)
    context = jnp.einsum('bht,btl->bhl', weights.astype(jnp.float32), key_rows[:, :, :LAT].astype(jnp.float32))
    context = context.astype(jnp.bfloat16)
    values = jnp.einsum('bhl,hlv->bhv', context.astype(jnp.float32), w_uv.astype(jnp.float32))
    values = values.astype(jnp.bfloat16).reshape(ROWS_ATT, HEADS * VDIM)
    attn_sum = jnp.dot(values, w_out, preferred_element_type=jnp.float32)
    attended = (residual.astype(jnp.float32) + attn_sum).astype(jnp.bfloat16)
    wide = attended.astype(jnp.float32)
    mean_square = lax.optimization_barrier(jnp.mean(wide * wide, axis=-1, keepdims=True))
    normed = (wide / jnp.sqrt(mean_square + 1e-06) * norm_gain).astype(jnp.bfloat16)
    hidden = jax.nn.silu(jnp.dot(normed, w_gate, preferred_element_type=jnp.float32)).astype(jnp.bfloat16)
    ffn_sum = jnp.dot(hidden, w_down, preferred_element_type=jnp.float32)
    ffn_out = (wide + ffn_sum).astype(jnp.bfloat16)
    return (attended, ffn_out)
```

```python
import jax
import jax.numpy as jnp
from jax import lax
from jax.experimental import pallas as pl
from jax.experimental.pallas import tpu as pltpu
from jax.sharding import PartitionSpec as P

SCALE = 0.07216878364870322
LAT = 512
KW = 576
D = 3584
HALF = 1792
CH = 896
FFL = 576
Z = 8
BF = jnp.bfloat16
F32 = jnp.float32
MESH = pl.DeviceIdType.MESH

PIECES = [(d, k, dist) for d in (0, 1) for k in (0, 1) for dist in (4, 3, 2, 1) if dist < 4 or d == k]
PIX = {p: i for i, p in enumerate(PIECES)}
NP = len(PIECES)


def kernel(
    q_h, pool_h, pt, ln, res_h, wuv_h, wout_h, gain_h, wg_h, wd_h,
    att_o, ffn_o,
    qv, poolv, resv, wuvv, woutv, gainv, wgv, wdv,
    sctx, ctxb, rctx, lhs, vals,
    part, pss, psr, rsb, rrb, gown, goth, xin, sq, hid, res_s, res_r, att16, fin_s, fin_r, outx_s, outx_r,
    lsem, a2a_s, a2a_r, ps_ss, ps_rs, rg_ss, rg_rs, ag_ss, ag_rs, sb_ss, sb_rs, ex_ss, ex_rs,
):
    me = lax.axis_index("rank")
    z = lax.div(me, 2)
    c = lax.rem(me, 2)
    sib = me + 1 - 2 * c

    def chip(j):
        return lax.rem(z + j, Z)

    down = {"rank": chip(7) * 2 + c}
    up = {"rank": chip(1) * 2 + c}
    other = {"rank": sib}

    own_col = pl.multiple_of(c * HALF, 128)
    oth_col = pl.multiple_of((1 - c) * HALF, 128)

    copies = []

    def load(src, dst):
        cp = pltpu.make_async_copy(src, dst, lsem.at[len(copies)])
        copies.append(cp)
        cp.start()
        return cp

    l_q = load(q_h, qv)
    l_pool = load(pool_h, poolv)
    l_res = load(res_h, resv)
    l_wuv = load(wuv_h, wuvv)
    l_wout = [load(wout_h.at[:, pl.ds(o, HALF)], woutv.at[i]) for i, o in enumerate((oth_col, own_col))]
    l_gain = [load(gain_h.at[:, pl.ds(o, HALF)], gainv.at[i]) for i, o in enumerate((oth_col, own_col))]
    l_wg = [load(wg_h.at[pl.ds(o, HALF), :], wgv.at[i]) for i, o in enumerate((oth_col, own_col))]
    l_wd = [load(wd_h.at[:, pl.ds(o, HALF)], wdv.at[i]) for i, o in enumerate((oth_col, own_col))]

    barrier = pltpu.get_barrier_semaphore()
    for k in range(1, 16):
        pl.semaphore_signal(barrier, inc=1, device_id={"rank": lax.rem(me + k, 16)}, device_id_type=MESH)

    l_q.wait()
    l_pool.wait()
    col = lax.broadcasted_iota(jnp.int32, (64, 128), 1)
    for b in range(8):
        key = jnp.concatenate([poolv[pt[b, 0]], poolv[pt[b, 1]]], axis=0)
        s = lax.dot_general(qv[b], key, (((1,), (1,)), ((), ())), preferred_element_type=F32) * SCALE
        s = jnp.where(col < ln[b], s, F32(-1e30))
        p = jnp.exp(s - jnp.max(s, axis=-1, keepdims=True))
        w = (p / jnp.sum(p, axis=-1, keepdims=True)).astype(BF)
        ctx = jnp.dot(w, key[:, :LAT], preferred_element_type=F32)
        for i in range(4):
            sctx[i, pl.ds(b, 64, stride=8), :] = ctx[:, i * 128 : (i + 1) * 128]
    for i in range(4):
        ctxb[:, pl.ds(i * 128, 128)] = sctx[i].astype(BF)

    pl.semaphore_wait(barrier, 15)

    sends = []

    def remote(src, dst, ss, rs, dev):
        cp = pltpu.make_async_remote_copy(
            src_ref=src, dst_ref=dst, send_sem=ss, recv_sem=rs, device_id=dev, device_id_type=MESH
        )
        cp.start()
        sends.append(cp)
        return cp

    def arrived(dst, rs):
        pltpu.make_async_copy(dst, dst, rs).wait()

    for j in (4, 3, 5, 2, 6, 1, 7):
        for k in (0, 1):
            dst = chip(j) * 2 + k
            remote(
                ctxb.at[pl.ds(pl.multiple_of(dst * 32, 32), 32), :],
                rctx.at[(8 - j) % 8, c],
                a2a_s.at[j, k],
                a2a_r.at[(8 - j) % 8, c],
                {"rank": dst},
            )
    remote(
        ctxb.at[pl.ds(pl.multiple_of(sib * 32, 32), 32), :],
        rctx.at[0, c],
        a2a_s.at[0, 0],
        a2a_r.at[0, c],
        other,
    )
    rctx[0, c] = ctxb[pl.ds(pl.multiple_of(me * 32, 32), 32), :]

    l_res.wait()
    res_r[c] = resv[:, pl.ds(own_col, HALF)].astype(F32)
    res_s[...] = resv[:, pl.ds(oth_col, HALF)].astype(F32)
    remote(res_s, res_r.at[c], ex_ss.at[0], ex_rs.at[0], other)

    def unpack(j):
        for hp in (0, 1):
            lo = rctx[j, 0, pl.ds(hp * 16, 16), :].astype(F32)
            hi = rctx[j, 1, pl.ds(hp * 16, 16), :].astype(F32)
            for h in (0, 1):
                blk = jnp.concatenate([lo[h * 8 : h * 8 + 8], hi[h * 8 : h * 8 + 8]], axis=0)
                lhs[hp * 2 + h, pl.ds(j * 16, 16), :] = blk.astype(BF)

    arrived(rctx.at[0, 1 - c], a2a_r.at[0, 1 - c])
    unpack(0)
    for j in (1, 7, 2, 6, 3, 5, 4):
        for k in (0, 1):
            arrived(rctx.at[j, k], a2a_r.at[j, k])
        unpack(j)

    l_wuv.wait()
    for h in range(4):
        v = jnp.dot(lhs[h], wuvv[h], preferred_element_type=F32)
        vals[:, pl.ds(h * 128, 128)] = v.astype(BF)

    def reduce_scatter(t, left, weights, loads):
        for w in loads:
            w.wait()
        for k in (0, 1):
            o = jnp.dot(left[...], weights[0, :, pl.ds(k * CH, CH)], preferred_element_type=F32)
            pss[t, k] = o.astype(BF)
            remote(pss.at[t, k], psr.at[t, k], ps_ss.at[t, k], ps_rs.at[t, k], other)
        for k in (0, 1):
            part[k] = jnp.dot(left[...], weights[1, :, pl.ds(k * CH, CH)], preferred_element_type=F32)

        def chip_sum(k, slot):
            rows = pl.ds(slot * 16, 16)
            return part[k, rows, :] + psr[t, k, rows, :].astype(F32)

        def step(d, k, dist):
            i = PIX[(d, k, dist)]
            slot = (8 - dist) if d == 0 else dist
            acc = chip_sum(k, slot)
            if (d, k, dist + 1) in PIX:
                prev = PIX[(d, k, dist + 1)]
                arrived(rrb.at[t, prev], rg_rs.at[t, prev])
                acc = acc + rrb[t, prev].astype(F32)
            rsb[t, i] = acc.astype(BF)
            remote(rsb.at[t, i], rrb.at[t, i], rg_ss.at[t, i], rg_rs.at[t, i], down if d == 0 else up)

        arrived(psr.at[t, 0], ps_rs.at[t, 0])
        step(0, 0, 4)
        step(1, 0, 3)
        arrived(psr.at[t, 1], ps_rs.at[t, 1])
        step(1, 1, 4)
        step(0, 1, 3)
        for dist in (3, 2, 1):
            step(0, 0, dist)
            step(1, 1, dist)
            if dist > 1:
                step(1, 0, dist - 1)
                step(0, 1, dist - 1)
        out = []
        for k in (0, 1):
            acc = chip_sum(k, 0)
            for d in ((1, 0) if k == 0 else (0, 1)):
                i = PIX[(d, k, 1)]
                arrived(rrb.at[t, i], rg_rs.at[t, i])
                acc = acc + rrb[t, i].astype(F32)
            out.append(acc)
        return out

    attn = reduce_scatter(0, vals, woutv, l_wout)

    arrived(res_r.at[1 - c], ex_rs.at[0])
    for w in l_gain:
        w.wait()

    def prepare(src, half, slot, k):
        cols = pl.ds(k * CH, CH)
        rows = pl.ds(slot * 16, 16)
        v = src.astype(F32)
        xin[half, rows, cols] = (v * gainv[half, :, cols]).astype(BF)
        s = v * v
        tot = s[:, 0:128]
        for i in range(1, CH // 128):
            tot = tot + s[:, i * 128 : (i + 1) * 128]
        sq[rows, :] = sq[rows, :] + tot

    sq[...] = jnp.zeros_like(sq)

    def to_sibling(slot, k):
        remote(gown.at[slot, k], goth.at[slot, k], sb_ss.at[slot, k], sb_rs.at[slot, k], other)

    def forward(d, k, dist):
        if (d, k, dist) not in PIX:
            return
        i = PIX[(d, k, dist)]
        src = (dist - 1) if d == 0 else (9 - dist) % 8
        dst = dist if d == 0 else 8 - dist
        remote(gown.at[src, k], gown.at[dst, k], ag_ss.at[i], ag_rs.at[i], down if d == 0 else up)

    for k in (0, 1):
        res = jnp.concatenate([res_r[0, :, k * CH : (k + 1) * CH], res_r[1, :, k * CH : (k + 1) * CH]], axis=0)
        att = (attn[k] + res).astype(BF)
        gown[0, k] = att
        forward(0, k, 1)
        forward(1, k, 1)
        to_sibling(0, k)
        att16[:, pl.ds(k * CH, CH)] = att.astype(F32)
    outx_s[0] = att16[pl.ds(pl.multiple_of((1 - c) * 8, 8), 8), :]
    remote(outx_s.at[0], outx_r.at[0], ex_ss.at[1], ex_rs.at[1], other)
    for k in (0, 1):
        prepare(gown[0, k], 1, 0, k)

    for dist in (1, 2, 3, 4):
        for k in (0, 1):
            for d in (0, 1):
                if (d, k, dist) not in PIX:
                    continue
                i = PIX[(d, k, dist)]
                slot = dist if d == 0 else 8 - dist
                arrived(gown.at[slot, k], ag_rs.at[i])
                forward(d, k, dist + 1)
                to_sibling(slot, k)
                prepare(gown[slot, k], 1, slot, k)
        for slot in sorted({dist - 1, (9 - dist) % 8}):
            for k in (0, 1):
                arrived(goth.at[slot, k], sb_rs.at[slot, k])
                prepare(goth[slot, k], 0, slot, k)
    for w in l_wg:
        w.wait()
    acc = jnp.dot(xin[1], wgv[1], preferred_element_type=F32)
    for k in (0, 1):
        arrived(goth.at[4, k], sb_rs.at[4, k])
        prepare(goth[4, k], 0, 4, k)
    acc = acc + jnp.dot(xin[0], wgv[0], preferred_element_type=F32)
    inv = lax.rsqrt(jnp.sum(sq[...], axis=-1, keepdims=True) * F32(1.0 / D) + F32(1e-6))
    g = acc * inv
    hid[...] = (g / (1.0 + jnp.exp(-g))).astype(BF)

    ffn = reduce_scatter(1, hid, wdv, l_wd)
    for k in (0, 1):
        cols = pl.ds(k * CH, CH)
        fin_s[:, cols] = (att16[:, cols] + ffn[k]).astype(BF).astype(F32)
    outx_s[1] = fin_s[pl.ds(pl.multiple_of((1 - c) * 8, 8), 8), :]
    remote(outx_s.at[1], outx_r.at[1], ex_ss.at[2], ex_rs.at[2], other)
    mine = pl.ds(pl.multiple_of(c * 8, 8), 8)
    att_o[:, pl.ds(own_col, HALF)] = att16[mine, :].astype(BF)
    ffn_o[:, pl.ds(own_col, HALF)] = fin_s[mine, :].astype(BF)
    arrived(outx_r.at[0], ex_rs.at[1])
    att_o[:, pl.ds(oth_col, HALF)] = outx_r[0].astype(BF)
    arrived(outx_r.at[1], ex_rs.at[2])
    ffn_o[:, pl.ds(oth_col, HALF)] = outx_r[1].astype(BF)
    for cp in sends:
        cp.wait_send()


def body(queries, cache_pool, page_table, lengths, residual, w_uv, w_out, norm_gain, w_gate, w_down):
    anyspec = pl.BlockSpec(memory_space=pl.ANY)
    smem = pl.BlockSpec(memory_space=pltpu.SMEM)
    vmem = pl.BlockSpec(memory_space=pltpu.VMEM)
    V = pltpu.VMEM
    DMA = pltpu.SemaphoreType.DMA
    return pl.pallas_call(
        kernel,
        out_shape=(jax.ShapeDtypeStruct((8, D), BF), jax.ShapeDtypeStruct((8, D), BF)),
        in_specs=[anyspec, anyspec, smem, smem] + [anyspec] * 6,
        out_specs=(vmem, vmem),
        scratch_shapes=[
            V((8, 64, KW), BF), V((16, 64, KW), BF), V((8, D), BF), V((4, LAT, 128), BF),
            V((2, 512, HALF), BF), V((2, 1, HALF), F32), V((2, HALF, FFL), BF), V((2, FFL, HALF), BF),
            V((4, 512, 128), F32), V((512, LAT), BF), V((Z, 2, 32, LAT), BF), V((4, 128, LAT), BF), V((128, 512), BF),
            V((2, 128, CH), F32), V((2, 2, 128, CH), BF), V((2, 2, 128, CH), BF),
            V((2, NP, 16, CH), BF), V((2, NP, 16, CH), BF),
            V((Z, 2, 16, CH), BF), V((Z, 2, 16, CH), BF), V((2, 128, HALF), BF), V((128, 128), F32), V((128, FFL), BF),
            V((8, HALF), F32), V((2, 8, HALF), F32), V((16, HALF), F32), V((16, HALF), F32), V((8, HALF), F32),
            V((2, 8, HALF), F32), V((2, 8, HALF), F32),
            DMA((12,)), DMA((Z, 2)), DMA((Z, 2)), DMA((2, 2)), DMA((2, 2)), DMA((2, NP)), DMA((2, NP)),
            DMA((NP,)), DMA((NP,)), DMA((Z, 2)), DMA((Z, 2)), DMA((3,)), DMA((3,)),
        ],
        compiler_params=pltpu.CompilerParams(
            collective_id=0, has_side_effects=True, vmem_limit_bytes=48 * 1024 * 1024
        ),
        cost_estimate=pl.CostEstimate(flops=1800000000, bytes_accessed=14400000, transcendentals=100000),
    )(queries, cache_pool, page_table, lengths, residual, w_uv, w_out, norm_gain.reshape(1, D), w_gate, w_down)


def solution(mesh):
    return jax.shard_map(
        body,
        mesh=mesh,
        in_specs=(
            P(("grp", "rank"), None, None),
            P(("grp", "rank"), None, None),
            P(("grp", "rank"), None),
            P(("grp", "rank")),
            P(("grp", "rank"), None),
            P("rank", None, None),
            P("rank", None),
            P(),
            P(None, "rank"),
            P("rank", None),
        ),
        out_specs=(P(("grp", "rank"), None), P(("grp", "rank"), None)),
        check_vma=False,
    )
```

```python
import jax
import jax.numpy as jnp
from jax import lax
from jax.experimental import pallas as pl
from jax.experimental.pallas import tpu as pltpu
from jax.sharding import PartitionSpec as P

SCALE = 0.07216878364870322
LAT = 512
KW = 576
D = 3584
HALF = 1792
CH = 896
FFL = 576
Z = 8
NB = 2
BF = jnp.bfloat16
F32 = jnp.float32
NT = (((1,), (1,)), ((), ()))
MESH = pl.DeviceIdType.MESH
FAR = (4, 3, 5, 2, 6, 1, 7)


def kernel(
    q_h, pool_h, pt, ln, res_h, wuv_h, wout_h, gain_h, wg_h, wd_h,
    att_o, ffn_o,
    qv, poolv, resv, wuvv, woutv, gain1, gain2, gainv, wgv, wdv,
    ctxa, ctxb, rctx, lhs, vals,
    part, pss, psr, rsb, rrb, gown, goth, xin, sq, hid, res_s, res_r, att, fin, outx_r,
    lsem, a2a_s, a2a_r, ps_ss, ps_rs, rg_ss, rg_rs, ag_ss, ag_rs, sb_ss, sb_rs, ex_ss, ex_rs,
):
    me = lax.axis_index("rank")
    z = lax.div(me, 2)
    c = lax.rem(me, 2)
    sib = me + 1 - 2 * c
    other = {"rank": sib}

    def chip(j):
        return lax.rem(z + j, Z)

    own_col = pl.multiple_of(c * HALF, 128)
    oth_col = pl.multiple_of((1 - c) * HALF, 128)

    copies = []
    sends = []

    def load(src, dst):
        cp = pltpu.make_async_copy(src, dst, lsem.at[len(copies)])
        copies.append(cp)
        cp.start()
        return cp

    l_q = [load(q_h.at[pl.ds(4 * i, 4)], qv.at[pl.ds(4 * i, 4)]) for i in range(NB)]
    l_pool = load(pool_h, poolv)
    l_res = load(res_h, resv)
    l_gain = load(gain_h, gain1)
    l_wuv = load(wuv_h, wuvv)
    l_wout = [load(wout_h.at[:, pl.ds(o, HALF)], woutv.at[i]) for i, o in enumerate((oth_col, own_col))]
    l_wg = [load(wg_h.at[:, pl.ds(o, HALF)], wgv.at[i]) for i, o in enumerate((oth_col, own_col))]
    l_wd = [load(wd_h.at[:, pl.ds(o, HALF)], wdv.at[i]) for i, o in enumerate((oth_col, own_col))]

    barrier = pltpu.get_barrier_semaphore()
    for k in range(1, 16):
        pl.semaphore_signal(barrier, inc=1, device_id={"rank": lax.rem(me + k, 16)}, device_id_type=MESH)

    def remote(src, dst, ss, rs, dev):
        cp = pltpu.make_async_remote_copy(
            src_ref=src, dst_ref=dst, send_sem=ss, recv_sem=rs, device_id=dev, device_id_type=MESH
        )
        cp.start()
        sends.append(cp)

    def arrived(dst, rs):
        pltpu.make_async_copy(dst, dst, rs).wait()

    ri = lax.broadcasted_iota(jnp.int32, (256, 256), 0)
    ci = lax.broadcasted_iota(jnp.int32, (256, 256), 1)
    to_rank = (ci == ((ri >> 2) & 3) * 64 + (ri >> 4) * 4 + (ri & 3)).astype(F32).astype(BF)
    to_head = (ci == (ri & 63) * 4 + (ri >> 6)).astype(F32).astype(BF)
    col = lax.broadcasted_iota(jnp.int32, (64, 128), 1)

    def attend(i):
        for r in range(4):
            b = 4 * i + r
            key = jnp.concatenate([poolv[pt[0, b]], poolv[pt[1, b]]], axis=0)
            s = lax.dot_general(qv[b], key, NT, preferred_element_type=F32) * SCALE
            s = jnp.where(col < ln[b], s, F32(-1e30))
            p = jnp.exp(s - jnp.max(s, axis=-1, keepdims=True))
            w = (p / jnp.sum(p, axis=-1, keepdims=True)).astype(BF)
            ctxa[i, pl.ds(r * 64, 64), :] = jnp.dot(w, key[:, :LAT], preferred_element_type=F32).astype(BF)
        ctxb[i] = jnp.dot(to_rank, ctxa[i], preferred_element_type=F32).astype(BF)

    def send_contexts(i):
        def block(rank):
            return pl.ds(pl.multiple_of(rank * 16, 16), 16)

        for j in FAR:
            for k in (0, 1):
                dst = chip(j) * 2 + k
                remote(
                    ctxb.at[i, block(dst), :], rctx.at[i, 8 - j, c], a2a_s.at[i, j, k], a2a_r.at[i, 8 - j, c], {"rank": dst}
                )
        remote(ctxb.at[i, block(sib), :], rctx.at[i, 0, c], a2a_s.at[i, 0, 0], a2a_r.at[i, 0, c], other)
        rctx[i, 0, c] = ctxb[i, block(me), :]

    def project(i):
        arrived(rctx.at[i, 0, 1 - c], a2a_r.at[i, 0, 1 - c])
        for j in FAR:
            for k in (0, 1):
                arrived(rctx.at[i, j, k], a2a_r.at[i, j, k])
        lhs[i] = jnp.dot(to_head, rctx[i].reshape(256, LAT), preferred_element_type=F32).astype(BF)
        for h in range(4):
            v = jnp.dot(lhs[i, pl.ds(h * 64, 64), :], wuvv[h], preferred_element_type=F32)
            vals[i, :, pl.ds(h * 128, 128)] = v.astype(BF)

    def pair_start(t, i, left, weights):
        for k in (0, 1):
            o = jnp.dot(left, weights[0, :, pl.ds(k * CH, CH)], preferred_element_type=F32)
            pss[t, i, k] = o.astype(BF)
            remote(pss.at[t, i, k], psr.at[t, i, k], ps_ss.at[t, i, k], ps_rs.at[t, i, k], other)
        for k in (0, 1):
            part[t, i, k] = jnp.dot(left, weights[1, :, pl.ds(k * CH, CH)], preferred_element_type=F32)

    def scatter_start(t, i):
        for k in (0, 1):
            arrived(psr.at[t, i, k], ps_rs.at[t, i, k])
            part[t, i, k] = part[t, i, k] + psr[t, i, k].astype(F32)
        for j in FAR:
            rows = pl.ds(8 * j, 8)
            rsb[t, i, j] = jnp.concatenate([part[t, i, 0, rows, :], part[t, i, 1, rows, :]], axis=0).astype(BF)
            remote(
                rsb.at[t, i, j], rrb.at[t, i, 8 - j], rg_ss.at[t, i, j], rg_rs.at[t, i, 8 - j], {"rank": chip(j) * 2 + c}
            )

    def scatter_end(t, i):
        acc = jnp.concatenate([part[t, i, 0, pl.ds(0, 8), :], part[t, i, 1, pl.ds(0, 8), :]], axis=0)
        for j in FAR:
            arrived(rrb.at[t, i, j], rg_rs.at[t, i, j])
            acc = acc + rrb[t, i, j].astype(F32)
        return acc

    def prepare(i, src, half, slot):
        rows = pl.ds(slot * 8, 8)
        v = src.astype(F32)
        tot = jnp.zeros((8, 128), F32)
        for k in (0, 1):
            u = v[8 * k : 8 * k + 8]
            xin[i, half, rows, pl.ds(k * CH, CH)] = u * gainv[half, :, pl.ds(k * CH, CH)]
            u = u * u
            for n in range(CH // 128):
                tot = tot + u[:, n * 128 : (n + 1) * 128]
        sq[i, half, rows, :] = tot

    def gather_start(i, attn):
        res = jnp.concatenate(
            [res_r[c2, 4 * i : 4 * i + 4, k * CH : (k + 1) * CH] for k in (0, 1) for c2 in (0, 1)], axis=0
        )
        a = (attn + res).astype(BF)
        gown[i, 0] = a
        for j in FAR:
            remote(gown.at[i, 0], gown.at[i, 8 - j], ag_ss.at[i, j], ag_rs.at[i, 8 - j], {"rank": chip(j) * 2 + c})
        remote(gown.at[i, 0], goth.at[i, 0], sb_ss.at[i, 0], sb_rs.at[i, 0], other)
        att[0, i] = a.astype(F32)
        remote(att.at[0, i], outx_r.at[0, i], ex_ss.at[1, i], ex_rs.at[1, i], other)
        prepare(i, a, 1, 0)

    def gather_end(i):
        for j in FAR:
            arrived(gown.at[i, j], ag_rs.at[i, j])
            remote(gown.at[i, j], goth.at[i, j], sb_ss.at[i, j], sb_rs.at[i, j], other)
            prepare(i, gown[i, j], 1, j)
        acc = lax.dot_general(xin[i, 1].astype(BF), wgv[1], NT, preferred_element_type=F32)
        for j in (0,) + FAR:
            arrived(goth.at[i, j], sb_rs.at[i, j])
            prepare(i, goth[i, j], 0, j)
        acc = acc + lax.dot_general(xin[i, 0].astype(BF), wgv[0], NT, preferred_element_type=F32)
        ms = jnp.sum(sq[i, 0] + sq[i, 1], axis=-1, keepdims=True) * F32(1.0 / D)
        g = acc * lax.rsqrt(ms + F32(1e-6))
        hid[i] = (g / (1.0 + jnp.exp(-g))).astype(BF)

    l_pool.wait()
    for i in range(NB):
        l_q[i].wait()
        attend(i)
        if i == 0:
            pl.semaphore_wait(barrier, 15)
        send_contexts(i)

    l_res.wait()
    res_r[c] = resv[:, pl.ds(own_col, HALF)].astype(F32)
    res_s[...] = resv[:, pl.ds(oth_col, HALF)].astype(F32)
    remote(res_s, res_r.at[c], ex_ss.at[0, 0], ex_rs.at[0, 0], other)
    l_gain.wait()
    gain2[...] = gain1[...].reshape(1, D)
    gainv[0] = gain2[:, pl.ds(oth_col, HALF)]
    gainv[1] = gain2[:, pl.ds(own_col, HALF)]

    l_wuv.wait()
    for w in l_wout:
        w.wait()
    for i in range(NB):
        project(i)
        pair_start(0, i, vals[i], woutv)
        scatter_start(0, i)
    arrived(res_r.at[1 - c], ex_rs.at[0, 0])
    for i in range(NB):
        gather_start(i, scatter_end(0, i))
    for w in l_wg + l_wd:
        w.wait()
    for i in range(NB):
        gather_end(i)
        pair_start(1, i, hid[i], wdv)
        scatter_start(1, i)
    for i in range(NB):
        fin[i] = (att[0, i] + scatter_end(1, i)).astype(BF).astype(F32)
        remote(fin.at[i], outx_r.at[1, i], ex_ss.at[2, i], ex_rs.at[2, i], other)

    def rows_of(blocks, k):
        parts = []
        for i in range(NB):
            v = blocks[i]
            parts.append(jnp.where(c == 0, v[8 * k : 8 * k + 4], v[8 * k + 4 : 8 * k + 8]))
        return jnp.concatenate(parts, axis=0).astype(BF)

    for k in (0, 1):
        att_o[:, pl.ds(pl.multiple_of(own_col + k * CH, 128), CH)] = rows_of([att[0, i] for i in range(NB)], k)
        ffn_o[:, pl.ds(pl.multiple_of(own_col + k * CH, 128), CH)] = rows_of([fin[i] for i in range(NB)], k)
    for t, o in ((0, att_o), (1, ffn_o)):
        for i in range(NB):
            arrived(outx_r.at[t, i], ex_rs.at[t + 1, i])
        for k in (0, 1):
            o[:, pl.ds(pl.multiple_of(oth_col + k * CH, 128), CH)] = rows_of([outx_r[t, i] for i in range(NB)], k)
    for cp in sends:
        cp.wait_send()


def body(queries, cache_pool, page_table, lengths, residual, w_uv, w_out, norm_gain, w_gate, w_down):
    anyspec = pl.BlockSpec(memory_space=pl.ANY)
    smem = pl.BlockSpec(memory_space=pltpu.SMEM)
    vmem = pl.BlockSpec(memory_space=pltpu.VMEM)
    V = pltpu.VMEM
    DMA = pltpu.SemaphoreType.DMA
    return pl.pallas_call(
        kernel,
        out_shape=(jax.ShapeDtypeStruct((8, D), BF), jax.ShapeDtypeStruct((8, D), BF)),
        in_specs=[anyspec, anyspec, smem, smem] + [anyspec] * 6,
        out_specs=(vmem, vmem),
        scratch_shapes=[
            V((8, 64, KW), BF), V((16, 64, KW), BF), V((8, D), BF), V((4, LAT, 128), BF),
            V((2, 512, HALF), BF), V((D,), F32), V((1, D), F32), V((2, 1, HALF), F32), V((2, FFL, HALF), BF), V((2, FFL, HALF), BF),
            V((NB, 256, LAT), BF), V((NB, 256, LAT), BF), V((NB, Z, 2, 16, LAT), BF), V((NB, 256, LAT), BF), V((NB, 64, 512), BF),
            V((2, NB, 2, 64, CH), F32), V((2, NB, 2, 64, CH), BF), V((2, NB, 2, 64, CH), BF),
            V((2, NB, Z, 16, CH), BF), V((2, NB, Z, 16, CH), BF),
            V((NB, Z, 16, CH), BF), V((NB, Z, 16, CH), BF), V((NB, 2, 64, HALF), F32), V((NB, 2, 64, 128), F32), V((NB, 64, FFL), BF),
            V((8, HALF), F32), V((2, 8, HALF), F32), V((1, NB, 16, CH), F32), V((NB, 16, CH), F32), V((2, NB, 16, CH), F32),
            DMA((16,)), DMA((NB, Z, 2)), DMA((NB, Z, 2)), DMA((2, NB, 2)), DMA((2, NB, 2)), DMA((2, NB, Z)), DMA((2, NB, Z)),
            DMA((NB, Z)), DMA((NB, Z)), DMA((NB, Z)), DMA((NB, Z)), DMA((3, NB)), DMA((3, NB)),
        ],
        compiler_params=pltpu.CompilerParams(
            collective_id=0, has_side_effects=True, vmem_limit_bytes=60 * 1024 * 1024
        ),
        cost_estimate=pl.CostEstimate(flops=1800000000, bytes_accessed=14400000, transcendentals=100000),
    )(queries, cache_pool, page_table.T, lengths, residual, w_uv, w_out, norm_gain, w_gate.T, w_down)


def solution(mesh):
    return jax.shard_map(
        body,
        mesh=mesh,
        in_specs=(
            P(("grp", "rank"), None, None),
            P(("grp", "rank"), None, None),
            P(("grp", "rank"), None),
            P(("grp", "rank")),
            P(("grp", "rank"), None),
            P("rank", None, None),
            P("rank", None),
            P(),
            P(None, "rank"),
            P("rank", None),
        ),
        out_specs=(P(("grp", "rank"), None), P(("grp", "rank"), None)),
        check_vma=False,
    )
```

```python
import jax
import jax.numpy as jnp
from jax import lax
from jax.experimental import pallas as pl
from jax.experimental.pallas import tpu as pltpu
from jax.sharding import PartitionSpec as P

SCALE = 0.07216878364870322
LAT = 512
KW = 576
D = 3584
HALF = 1792
CH = 896
FFL = 576
Z = 8
NB = 2
BF = jnp.bfloat16
F32 = jnp.float32
NT = (((1,), (1,)), ((), ()))
MESH = pl.DeviceIdType.MESH
FAR = (4, 3, 5, 2, 6, 1, 7)


def kernel(
    q_h, pool_h, pt, ln, res_h, wuv_h, wout_h, gain_h, wg_h, wd_h,
    att_o, ffn_o,
    qv, poolv, resv, wuvv, woutv, gain1, gain2, gainv, wgv, wdv,
    ctxa, ctxb, rctx, lhs, vals,
    part, rsb, rrb, gown, xin, sq, pre, hid, res_s, res_r, att, fin, outx_r,
    lsem, a2a_s, a2a_r, w_ss, w_rs, v_ss, v_rs, rg_ss, rg_rs, ag_ss, ag_rs, h_ss, h_rs, ex_ss, ex_rs,
):
    me = lax.axis_index("rank")
    z = lax.div(me, 2)
    c = lax.rem(me, 2)
    sib = me + 1 - 2 * c
    other = {"rank": sib}

    def chip(j):
        return lax.rem(z + j, Z)

    own_col = pl.multiple_of(c * HALF, 128)
    oth_col = pl.multiple_of((1 - c) * HALF, 128)

    barrier = pltpu.get_barrier_semaphore()
    for k in (8, 9, 7, 6, 10, 5, 11, 4, 12, 3, 13, 2, 14, 1, 15):
        pl.semaphore_signal(barrier, inc=1, device_id={"rank": lax.rem(me + k, 16)}, device_id_type=MESH)

    copies = []
    sends = []

    def load(src, dst):
        cp = pltpu.make_async_copy(src, dst, lsem.at[len(copies)])
        copies.append(cp)
        cp.start()
        return cp

    l_q = [load(q_h.at[pl.ds(4 * i, 4)], qv.at[pl.ds(4 * i, 4)]) for i in range(NB)]
    l_pool = load(pool_h, poolv)
    l_res = load(res_h, resv)
    l_gain = load(gain_h, gain1)
    l_wuv = load(wuv_h, wuvv)
    l_wout = load(wout_h.at[:, pl.ds(own_col, HALF)], woutv.at[0])
    l_wg = load(wg_h.at[:, pl.ds(own_col, HALF)], wgv.at[0])
    l_wd = load(wd_h.at[:, pl.ds(own_col, HALF)], wdv.at[0])

    def remote(src, dst, ss, rs, dev):
        cp = pltpu.make_async_remote_copy(
            src_ref=src, dst_ref=dst, send_sem=ss, recv_sem=rs, device_id=dev, device_id_type=MESH
        )
        cp.start()
        sends.append(cp)

    def arrived(dst, rs):
        pltpu.make_async_copy(dst, dst, rs).wait()

    ri = lax.broadcasted_iota(jnp.int32, (256, 256), 0)
    ci = lax.broadcasted_iota(jnp.int32, (256, 256), 1)
    to_rank = (ci == ((ri >> 2) & 3) * 64 + (ri >> 4) * 4 + (ri & 3)).astype(F32).astype(BF)
    to_head = (ci == (ri & 63) * 4 + (ri >> 6)).astype(F32).astype(BF)
    col = lax.broadcasted_iota(jnp.int32, (64, 128), 1)

    def attend(i):
        for r in range(4):
            b = 4 * i + r
            key = jnp.concatenate([poolv[pt[0, b]], poolv[pt[1, b]]], axis=0)
            s = lax.dot_general(qv[b], key, NT, preferred_element_type=F32) * SCALE
            s = jnp.where(col < ln[b], s, F32(-1e30))
            p = jnp.exp(s - jnp.max(s, axis=-1, keepdims=True))
            w = (p / jnp.sum(p, axis=-1, keepdims=True)).astype(BF)
            ctxa[i, pl.ds(r * 64, 64), :] = jnp.dot(w, key[:, :LAT], preferred_element_type=F32).astype(BF)
        ctxb[i] = jnp.dot(to_rank, ctxa[i], preferred_element_type=F32).astype(BF)

    def send_contexts(i):
        def block(rank):
            return pl.ds(pl.multiple_of(rank * 16, 16), 16)

        for j in FAR:
            for k in (0, 1):
                dst = chip(j) * 2 + k
                remote(
                    ctxb.at[i, block(dst), :], rctx.at[i, 8 - j, c], a2a_s.at[i, j, k], a2a_r.at[i, 8 - j, c], {"rank": dst}
                )
        remote(ctxb.at[i, block(sib), :], rctx.at[i, 0, c], a2a_s.at[i, 0, 0], a2a_r.at[i, 0, c], other)
        rctx[i, 0, c] = ctxb[i, block(me), :]

    def project(i):
        arrived(rctx.at[i, 0, 1 - c], a2a_r.at[i, 0, 1 - c])
        for j in FAR:
            for k in (0, 1):
                arrived(rctx.at[i, j, k], a2a_r.at[i, j, k])
        lhs[i] = jnp.dot(to_head, rctx[i].reshape(256, LAT), preferred_element_type=F32).astype(BF)
        for h in range(4):
            v = jnp.dot(lhs[i, pl.ds(h * 64, 64), :], wuvv[h], preferred_element_type=F32)
            vals[i, 0, :, pl.ds(h * 128, 128)] = v.astype(BF)
        remote(vals.at[i, 0], vals.at[i, 1], v_ss.at[i], v_rs.at[i], other)

    def multiply(t, i, left, weights, ready):
        for k in (0, 1):
            part[t, i, k] = jnp.dot(left[i, 0], weights[0, :, pl.ds(k * CH, CH)], preferred_element_type=F32)
        if ready:
            arrived(left.at[i, 1], v_rs.at[i])
        for k in (0, 1):
            o = jnp.dot(left[i, 1], weights[1, :, pl.ds(k * CH, CH)], preferred_element_type=F32)
            part[t, i, k] = part[t, i, k] + o

    def scatter_start(t, i):
        for j in FAR:
            rows = pl.ds(8 * j, 8)
            rsb[t, i, j] = jnp.concatenate([part[t, i, 0, rows, :], part[t, i, 1, rows, :]], axis=0).astype(BF)
            remote(
                rsb.at[t, i, j], rrb.at[t, i, 8 - j], rg_ss.at[t, i, j], rg_rs.at[t, i, 8 - j], {"rank": chip(j) * 2 + c}
            )

    def scatter_end(t, i):
        acc = jnp.concatenate([part[t, i, 0, pl.ds(0, 8), :], part[t, i, 1, pl.ds(0, 8), :]], axis=0)
        for j in FAR:
            arrived(rrb.at[t, i, j], rg_rs.at[t, i, j])
            acc = acc + rrb[t, i, j].astype(F32)
        return acc

    def prepare(i, src, slot):
        rows = pl.ds(slot * 8, 8)
        v = src.astype(F32)
        tot = jnp.zeros((8, 128), F32)
        for k in (0, 1):
            u = v[8 * k : 8 * k + 8]
            xin[i, rows, pl.ds(k * CH, CH)] = u * gainv[:, pl.ds(k * CH, CH)]
            u = u * u
            for n in range(CH // 128):
                tot = tot + u[:, n * 128 : (n + 1) * 128]
        sq[i, 0, rows, :] = tot

    def gather_start(i, attn):
        res = jnp.concatenate(
            [res_r[c2, 4 * i : 4 * i + 4, k * CH : (k + 1) * CH] for k in (0, 1) for c2 in (0, 1)], axis=0
        )
        a = (attn + res).astype(BF)
        gown[i, 0] = a
        for j in FAR:
            remote(gown.at[i, 0], gown.at[i, 8 - j], ag_ss.at[i, j], ag_rs.at[i, 8 - j], {"rank": chip(j) * 2 + c})
        att[0, i] = a.astype(F32)
        remote(att.at[0, i], outx_r.at[0, i], ex_ss.at[1, i], ex_rs.at[1, i], other)
        prepare(i, a, 0)

    def gather_end(i):
        for j in FAR:
            arrived(gown.at[i, j], ag_rs.at[i, j])
            prepare(i, gown[i, j], j)
        remote(sq.at[i, 0], sq.at[i, 1], h_ss.at[i, 2], h_rs.at[i, 2], other)
        x = xin[i].astype(BF)
        for u in (1, 0):
            pre[i, 0, u] = lax.dot_general(x, wgv[u], NT, preferred_element_type=F32).astype(BF)
            remote(pre.at[i, 0, u], pre.at[i, 1, 1 - u], h_ss.at[i, u], h_rs.at[i, 1 - u], other)

    def activate(i):
        arrived(sq.at[i, 1], h_rs.at[i, 2])
        ms = jnp.sum(sq[i, 0] + sq[i, 1], axis=-1, keepdims=True) * F32(1.0 / D)
        inv = lax.rsqrt(ms + F32(1e-6))
        for u in (0, 1):
            arrived(pre.at[i, 1, u], h_rs.at[i, u])
            g = (pre[i, 0, u].astype(F32) + pre[i, 1, u].astype(F32)) * inv
            hid[i, u] = (g / (1.0 + jnp.exp(-g))).astype(BF)

    def push(src, dst, n):
        remote(src.at[:, pl.ds(oth_col, HALF)], dst.at[1], w_ss.at[n], w_rs.at[n], other)

    l_pool.wait()
    l_q[0].wait()
    attend(0)
    pl.semaphore_wait(barrier, 15)
    push(wout_h, woutv, 0)
    push(wg_h, wgv, 1)
    push(wd_h, wdv, 2)
    send_contexts(0)
    l_q[1].wait()
    attend(1)
    send_contexts(1)

    l_res.wait()
    res_r[c] = resv[:, pl.ds(own_col, HALF)].astype(F32)
    res_s[...] = resv[:, pl.ds(oth_col, HALF)].astype(F32)
    remote(res_s, res_r.at[c], ex_ss.at[0, 0], ex_rs.at[0, 0], other)
    l_gain.wait()
    gain2[...] = gain1[...].reshape(1, D)
    gainv[...] = gain2[:, pl.ds(own_col, HALF)]

    l_wuv.wait()
    l_wout.wait()
    arrived(woutv.at[1], w_rs.at[0])

    def finish(i):
        fin[i] = (att[0, i] + scatter_end(1, i)).astype(BF).astype(F32)
        remote(fin.at[i], outx_r.at[1, i], ex_ss.at[2, i], ex_rs.at[2, i], other)

    for i in range(NB):
        project(i)
        multiply(0, i, vals, woutv, True)
        scatter_start(0, i)
    arrived(res_r.at[1 - c], ex_rs.at[0, 0])
    for i in range(NB):
        gather_start(i, scatter_end(0, i))
    l_wg.wait()
    arrived(wgv.at[1], w_rs.at[1])
    l_wd.wait()
    arrived(wdv.at[1], w_rs.at[2])
    for i in range(NB):
        gather_end(i)
        activate(i)
        multiply(1, i, hid, wdv, False)
        scatter_start(1, i)
    for i in range(NB):
        finish(i)

    def rows_of(blocks, k):
        parts = []
        for i in range(NB):
            v = blocks[i]
            parts.append(jnp.where(c == 0, v[8 * k : 8 * k + 4], v[8 * k + 4 : 8 * k + 8]))
        return jnp.concatenate(parts, axis=0).astype(BF)

    for k in (0, 1):
        att_o[:, pl.ds(pl.multiple_of(own_col + k * CH, 128), CH)] = rows_of([att[0, i] for i in range(NB)], k)
        ffn_o[:, pl.ds(pl.multiple_of(own_col + k * CH, 128), CH)] = rows_of([fin[i] for i in range(NB)], k)
    for t, o in ((0, att_o), (1, ffn_o)):
        for i in range(NB):
            arrived(outx_r.at[t, i], ex_rs.at[t + 1, i])
        for k in (0, 1):
            o[:, pl.ds(pl.multiple_of(oth_col + k * CH, 128), CH)] = rows_of([outx_r[t, i] for i in range(NB)], k)
    for cp in sends:
        cp.wait_send()


def keep(a, b, att_o, ffn_o):
    att_o[...] = a[...]
    ffn_o[...] = b[...]


def body(queries, cache_pool, page_table, lengths, residual, w_uv, w_out, norm_gain, w_gate, w_down):
    anyspec = pl.BlockSpec(memory_space=pl.ANY)
    smem = pl.BlockSpec(memory_space=pltpu.SMEM)
    vmem = pl.BlockSpec(memory_space=pltpu.VMEM)
    V = pltpu.VMEM
    DMA = pltpu.SemaphoreType.DMA
    att, ffn = pl.pallas_call(
        kernel,
        out_shape=(jax.ShapeDtypeStruct((8, D), BF), jax.ShapeDtypeStruct((8, D), BF)),
        in_specs=[anyspec, anyspec, smem, smem] + [anyspec] * 6,
        out_specs=(vmem, vmem),
        scratch_shapes=[
            V((8, 64, KW), BF), V((16, 64, KW), BF), V((8, D), BF), V((4, LAT, 128), BF),
            V((2, 512, HALF), BF), V((D,), F32), V((1, D), F32), V((1, HALF), F32), V((2, FFL, HALF), BF), V((2, FFL, HALF), BF),
            V((NB, 256, LAT), BF), V((NB, 256, LAT), BF), V((NB, Z, 2, 16, LAT), BF), V((NB, 256, LAT), BF), V((NB, 2, 64, 512), BF),
            V((2, NB, 2, 64, CH), F32), V((2, NB, Z, 16, CH), BF), V((2, NB, Z, 16, CH), BF),
            V((NB, Z, 16, CH), BF), V((NB, 64, HALF), F32), V((NB, 2, 64, 128), F32), V((NB, 2, 2, 64, FFL), BF), V((NB, 2, 64, FFL), BF),
            V((8, HALF), F32), V((2, 8, HALF), F32), V((1, NB, 16, CH), F32), V((NB, 16, CH), F32), V((2, NB, 16, CH), F32),
            DMA((16,)), DMA((NB, Z, 2)), DMA((NB, Z, 2)), DMA((3,)), DMA((3,)), DMA((NB,)), DMA((NB,)), DMA((2, NB, Z)), DMA((2, NB, Z)),
            DMA((NB, Z)), DMA((NB, Z)), DMA((NB, 3)), DMA((NB, 3)), DMA((3, NB)), DMA((3, NB)),
        ],
        compiler_params=pltpu.CompilerParams(
            collective_id=0, has_side_effects=True, vmem_limit_bytes=60 * 1024 * 1024
        ),
        cost_estimate=pl.CostEstimate(flops=1800000000, bytes_accessed=14400000, transcendentals=100000),
    )(queries, cache_pool, page_table.T, lengths, residual, w_uv, w_out, norm_gain, w_gate.T, w_down)
    return pl.pallas_call(
        keep,
        out_shape=(jax.ShapeDtypeStruct((8, D), BF), jax.ShapeDtypeStruct((8, D), BF)),
        in_specs=[vmem, vmem],
        out_specs=(vmem, vmem),
    )(att, ffn)


def solution(mesh):
    return jax.shard_map(
        body,
        mesh=mesh,
        in_specs=(
            P(("grp", "rank"), None, None),
            P(("grp", "rank"), None, None),
            P(("grp", "rank"), None),
            P(("grp", "rank")),
            P(("grp", "rank"), None),
            P("rank", None, None),
            P("rank", None),
            P(),
            P(None, "rank"),
            P("rank", None),
        ),
        out_specs=(P(("grp", "rank"), None), P(("grp", "rank"), None)),
        check_vma=False,
    )
```

```python
import jax
import jax.numpy as jnp
from jax import lax
from jax.experimental import pallas as pl
from jax.experimental.pallas import tpu as pltpu
from jax.sharding import PartitionSpec as P

SCALE = 0.07216878364870322
LAT = 512
KW = 576
D = 3584
HALF = 1792
CH = 896
FFL = 576
Z = 8
NB = 2
BF = jnp.bfloat16
F32 = jnp.float32
NT = (((1,), (1,)), ((), ()))
MESH = pl.DeviceIdType.MESH
FAR = (4, 3, 5, 2, 6, 1, 7)


def kernel(
    q_h, pool_h, pt, ln, res_h, wuv_h, wout_h, gain_h, wg_h, wd_h,
    att_o, ffn_o,
    qv, poolv, resv, wuvv, woutv, gain1, gain2, gainv, wgv, wdv,
    ctxa, ctxb, rctx, lhs, vals,
    part, rsb, rrb, gown, xin, sq, pre, hid, res_s, res_r, att, fin, outx_r,
    lsem, a2a_s, a2a_r, w_ss, w_rs, v_ss, v_rs, rg_ss, rg_rs, ag_ss, ag_rs, h_ss, h_rs, ex_ss, ex_rs,
):
    me = lax.axis_index("rank")
    z = lax.div(me, 2)
    c = lax.rem(me, 2)
    sib = me + 1 - 2 * c
    other = {"rank": sib}
    odd = lax.rem(z, 2)
    two = 2 + 4 * odd

    def chip(j):
        return lax.rem(z + j, Z)

    own_col = pl.multiple_of(c * HALF, 128)
    oth_col = pl.multiple_of((1 - c) * HALF, 128)

    barrier = pltpu.get_barrier_semaphore()
    for k in (8, 9, 7, 6, 10, 5, 11, 4, 12, 3, 13, 2, 14, 1, 15):
        pl.semaphore_signal(barrier, inc=1, device_id={"rank": lax.rem(me + k, 16)}, device_id_type=MESH)

    copies = []
    sends = []

    def load(src, dst):
        cp = pltpu.make_async_copy(src, dst, lsem.at[len(copies)])
        copies.append(cp)
        cp.start()
        return cp

    l_q = [load(q_h.at[pl.ds(4 * i, 4)], qv.at[pl.ds(4 * i, 4)]) for i in range(NB)]
    l_pool = load(pool_h, poolv)
    l_res = load(res_h, resv)
    l_gain = load(gain_h, gain1)
    l_wuv = load(wuv_h, wuvv)
    l_wout = load(wout_h.at[:, pl.ds(own_col, HALF)], woutv.at[0])
    l_wg = load(wg_h.at[:, pl.ds(own_col, HALF)], wgv.at[0])
    l_wd = load(wd_h.at[:, pl.ds(own_col, HALF)], wdv.at[0])

    def remote(src, dst, ss, rs, dev):
        cp = pltpu.make_async_remote_copy(
            src_ref=src, dst_ref=dst, send_sem=ss, recv_sem=rs, device_id=dev, device_id_type=MESH
        )
        cp.start()
        sends.append(cp)

    def arrived(dst, rs):
        pltpu.make_async_copy(dst, dst, rs).wait()

    ri = lax.broadcasted_iota(jnp.int32, (256, 256), 0)
    ci = lax.broadcasted_iota(jnp.int32, (256, 256), 1)
    to_rank = (ci == ((ri >> 2) & 3) * 64 + (ri >> 4) * 4 + (ri & 3)).astype(F32).astype(BF)
    to_head = (ci == (ri & 63) * 4 + (ri >> 6)).astype(F32).astype(BF)
    col = lax.broadcasted_iota(jnp.int32, (64, 128), 1)

    def attend(i):
        for r in range(4):
            b = 4 * i + r
            key = jnp.concatenate([poolv[pt[0, b]], poolv[pt[1, b]]], axis=0)
            s = lax.dot_general(qv[b], key, NT, preferred_element_type=F32) * SCALE
            s = jnp.where(col < ln[b], s, F32(-1e30))
            p = jnp.exp(s - jnp.max(s, axis=-1, keepdims=True))
            w = (p / jnp.sum(p, axis=-1, keepdims=True)).astype(BF)
            ctxa[i, pl.ds(r * 64, 64), :] = jnp.dot(w, key[:, :LAT], preferred_element_type=F32).astype(BF)
        ctxb[i] = jnp.dot(to_rank, ctxa[i], preferred_element_type=F32).astype(BF)

    def send_contexts(i):
        def block(rank):
            return pl.ds(pl.multiple_of(rank * 16, 16), 16)

        for j in FAR:
            for k in (0, 1):
                dst = chip(j) * 2 + k
                remote(
                    ctxb.at[i, block(dst), :], rctx.at[i, 8 - j, c], a2a_s.at[i, j, k], a2a_r.at[i, 8 - j, c], {"rank": dst}
                )
        remote(ctxb.at[i, block(sib), :], rctx.at[i, 0, c], a2a_s.at[i, 0, 0], a2a_r.at[i, 0, c], other)
        rctx[i, 0, c] = ctxb[i, block(me), :]

    def project(i):
        arrived(rctx.at[i, 0, 1 - c], a2a_r.at[i, 0, 1 - c])
        for j in FAR:
            for k in (0, 1):
                arrived(rctx.at[i, j, k], a2a_r.at[i, j, k])
        lhs[i] = jnp.dot(to_head, rctx[i].reshape(256, LAT), preferred_element_type=F32).astype(BF)
        for h in range(4):
            v = jnp.dot(lhs[i, pl.ds(h * 64, 64), :], wuvv[h], preferred_element_type=F32)
            vals[i, 0, :, pl.ds(h * 128, 128)] = v.astype(BF)
        remote(vals.at[i, 0], vals.at[i, 1], v_ss.at[i], v_rs.at[i], other)

    def multiply(t, i, left, weights, ready):
        for k in (0, 1):
            part[t, i, k] = jnp.dot(left[i, 0], weights[0, :, pl.ds(k * CH, CH)], preferred_element_type=F32)
        if ready:
            arrived(left.at[i, 1], v_rs.at[i])
        for k in (0, 1):
            o = jnp.dot(left[i, 1], weights[1, :, pl.ds(k * CH, CH)], preferred_element_type=F32)
            part[t, i, k] = part[t, i, k] + o

    def scatter_send(t, i, j, slot, dst, extra):
        rows = pl.ds(8 * j, 8)
        acc = jnp.concatenate([part[t, i, 0, rows, :], part[t, i, 1, rows, :]], axis=0)
        for e in extra:
            acc = acc + e
        rsb[t, i, j] = acc.astype(BF)
        remote(
            rsb.at[t, i, j], rrb.at[t, i, slot], rg_ss.at[t, i, j], rg_rs.at[t, i, slot], {"rank": dst * 2 + c}
        )

    def relayed(t, i):
        return t == 0 and i == 1

    def scatter_start(t, i):
        if not relayed(t, i):
            for j in FAR:
                scatter_send(t, i, j, 8 - j, chip(j), ())
        else:
            scatter_send(t, i, 4, 4, chip(two), ())
            scatter_send(t, i, 3, 3, chip(1), ())
            scatter_send(t, i, 5, 5, chip(7), ())
            scatter_send(t, i, 1, 7, chip(1), ())
            scatter_send(t, i, 7, 1, chip(7), ())

    def scatter_mid(t, i):
        arrived(rrb.at[t, i, 4], rg_rs.at[t, i, 4])
        far = rrb[t, i, 4].astype(F32)
        none = jnp.zeros_like(far)
        arrived(rrb.at[t, i, 3], rg_rs.at[t, i, 3])
        scatter_send(t, i, 2, 6, chip(2), (rrb[t, i, 3].astype(F32), jnp.where(odd == 0, far, none)))
        arrived(rrb.at[t, i, 5], rg_rs.at[t, i, 5])
        scatter_send(t, i, 6, 2, chip(6), (rrb[t, i, 5].astype(F32), jnp.where(odd == 0, none, far)))

    def scatter_end(t, i):
        acc = jnp.concatenate([part[t, i, 0, pl.ds(0, 8), :], part[t, i, 1, pl.ds(0, 8), :]], axis=0)
        for j in (1, 7, 2, 6) if relayed(t, i) else FAR:
            arrived(rrb.at[t, i, j], rg_rs.at[t, i, j])
            acc = acc + rrb[t, i, j].astype(F32)
        return acc

    def prepare(i, src, slot):
        rows = pl.ds(slot * 8, 8)
        v = src.astype(F32)
        tot = jnp.zeros((8, 128), F32)
        for k in (0, 1):
            u = v[8 * k : 8 * k + 8]
            xin[i, rows, pl.ds(k * CH, CH)] = u * gainv[:, pl.ds(k * CH, CH)]
            u = u * u
            for n in range(CH // 128):
                tot = tot + u[:, n * 128 : (n + 1) * 128]
        sq[i, 0, rows, :] = tot

    def gather_send(i, src, slot, dst):
        remote(gown.at[i, src], gown.at[i, slot], ag_ss.at[i, slot], ag_rs.at[i, slot], {"rank": dst * 2 + c})

    def gather_start(i, attn):
        res = jnp.concatenate(
            [res_r[c2, 4 * i : 4 * i + 4, k * CH : (k + 1) * CH] for k in (0, 1) for c2 in (0, 1)], axis=0
        )
        a = (attn + res).astype(BF)
        gown[i, 0] = a
        for j in FAR:
            gather_send(i, 0, 8 - j, chip(j))
        att[0, i] = a.astype(F32)
        remote(att.at[0, i], outx_r.at[0, i], ex_ss.at[1, i], ex_rs.at[1, i], other)
        prepare(i, a, 0)

    def gather_end(i):
        for j in FAR:
            arrived(gown.at[i, j], ag_rs.at[i, j])
            prepare(i, gown[i, j], j)
        remote(sq.at[i, 0], sq.at[i, 1], h_ss.at[i, 2], h_rs.at[i, 2], other)
        x = xin[i].astype(BF)
        for u in (1, 0):
            pre[i, 0, u] = lax.dot_general(x, wgv[u], NT, preferred_element_type=F32).astype(BF)
            remote(pre.at[i, 0, u], pre.at[i, 1, 1 - u], h_ss.at[i, u], h_rs.at[i, 1 - u], other)

    def activate(i):
        arrived(sq.at[i, 1], h_rs.at[i, 2])
        ms = jnp.sum(sq[i, 0] + sq[i, 1], axis=-1, keepdims=True) * F32(1.0 / D)
        inv = lax.rsqrt(ms + F32(1e-6))
        for u in (0, 1):
            arrived(pre.at[i, 1, u], h_rs.at[i, u])
            g = (pre[i, 0, u].astype(F32) + pre[i, 1, u].astype(F32)) * inv
            hid[i, u] = (g / (1.0 + jnp.exp(-g))).astype(BF)

    def push(src, dst, n):
        remote(src.at[:, pl.ds(oth_col, HALF)], dst.at[1], w_ss.at[n], w_rs.at[n], other)

    l_pool.wait()
    l_q[0].wait()
    attend(0)
    pl.semaphore_wait(barrier, 15)
    push(wout_h, woutv, 0)
    push(wg_h, wgv, 1)
    push(wd_h, wdv, 2)
    send_contexts(0)
    l_q[1].wait()
    attend(1)
    send_contexts(1)

    l_res.wait()
    res_r[c] = resv[:, pl.ds(own_col, HALF)].astype(F32)
    res_s[...] = resv[:, pl.ds(oth_col, HALF)].astype(F32)
    remote(res_s, res_r.at[c], ex_ss.at[0, 0], ex_rs.at[0, 0], other)
    l_gain.wait()
    gain2[...] = gain1[...].reshape(1, D)
    gainv[...] = gain2[:, pl.ds(own_col, HALF)]

    l_wuv.wait()
    l_wout.wait()
    arrived(woutv.at[1], w_rs.at[0])

    def finish(i):
        fin[i] = (att[0, i] + scatter_end(1, i)).astype(BF).astype(F32)
        remote(fin.at[i], outx_r.at[1, i], ex_ss.at[2, i], ex_rs.at[2, i], other)

    project(0)
    multiply(0, 0, vals, woutv, True)
    scatter_start(0, 0)
    project(1)
    multiply(0, 1, vals, woutv, True)
    scatter_start(0, 1)
    arrived(res_r.at[1 - c], ex_rs.at[0, 0])
    gather_start(0, scatter_end(0, 0))
    scatter_mid(0, 1)
    gather_start(1, scatter_end(0, 1))
    l_wg.wait()
    arrived(wgv.at[1], w_rs.at[1])
    l_wd.wait()
    arrived(wdv.at[1], w_rs.at[2])
    gather_end(0)
    activate(0)
    multiply(1, 0, hid, wdv, False)
    scatter_start(1, 0)
    gather_end(1)
    activate(1)
    multiply(1, 1, hid, wdv, False)
    scatter_start(1, 1)
    finish(0)
    finish(1)

    def rows_of(blocks, k):
        parts = []
        for i in range(NB):
            v = blocks[i]
            parts.append(jnp.where(c == 0, v[8 * k : 8 * k + 4], v[8 * k + 4 : 8 * k + 8]))
        return jnp.concatenate(parts, axis=0).astype(BF)

    for k in (0, 1):
        att_o[:, pl.ds(pl.multiple_of(own_col + k * CH, 128), CH)] = rows_of([att[0, i] for i in range(NB)], k)
        ffn_o[:, pl.ds(pl.multiple_of(own_col + k * CH, 128), CH)] = rows_of([fin[i] for i in range(NB)], k)
    for t, o in ((0, att_o), (1, ffn_o)):
        for i in range(NB):
            arrived(outx_r.at[t, i], ex_rs.at[t + 1, i])
        for k in (0, 1):
            o[:, pl.ds(pl.multiple_of(oth_col + k * CH, 128), CH)] = rows_of([outx_r[t, i] for i in range(NB)], k)
    for cp in sends:
        cp.wait_send()


def keep(a, b, att_o, ffn_o):
    att_o[...] = a[...]
    ffn_o[...] = b[...]


def body(queries, cache_pool, page_table, lengths, residual, w_uv, w_out, norm_gain, w_gate, w_down):
    anyspec = pl.BlockSpec(memory_space=pl.ANY)
    smem = pl.BlockSpec(memory_space=pltpu.SMEM)
    vmem = pl.BlockSpec(memory_space=pltpu.VMEM)
    V = pltpu.VMEM
    DMA = pltpu.SemaphoreType.DMA
    att, ffn = pl.pallas_call(
        kernel,
        out_shape=(V((8, D), BF), V((8, D), BF)),
        in_specs=[anyspec, anyspec, smem, smem] + [anyspec] * 6,
        out_specs=(vmem, vmem),
        scratch_shapes=[
            V((8, 64, KW), BF), V((16, 64, KW), BF), V((8, D), BF), V((4, LAT, 128), BF),
            V((2, 512, HALF), BF), V((D,), F32), V((1, D), F32), V((1, HALF), F32), V((2, FFL, HALF), BF), V((2, FFL, HALF), BF),
            V((NB, 256, LAT), BF), V((NB, 256, LAT), BF), V((NB, Z, 2, 16, LAT), BF), V((NB, 256, LAT), BF), V((NB, 2, 64, 512), BF),
            V((2, NB, 2, 64, CH), F32), V((2, NB, Z, 16, CH), BF), V((2, NB, Z, 16, CH), BF),
            V((NB, Z, 16, CH), BF), V((NB, 64, HALF), F32), V((NB, 2, 64, 128), F32), V((NB, 2, 2, 64, FFL), BF), V((NB, 2, 64, FFL), BF),
            V((8, HALF), F32), V((2, 8, HALF), F32), V((1, NB, 16, CH), F32), V((NB, 16, CH), F32), V((2, NB, 16, CH), F32),
            DMA((16,)), DMA((NB, Z, 2)), DMA((NB, Z, 2)), DMA((3,)), DMA((3,)), DMA((NB,)), DMA((NB,)), DMA((2, NB, Z)), DMA((2, NB, Z)),
            DMA((NB, Z)), DMA((NB, Z)), DMA((NB, 3)), DMA((NB, 3)), DMA((3, NB)), DMA((3, NB)),
        ],
        compiler_params=pltpu.CompilerParams(
            collective_id=0, has_side_effects=True, vmem_limit_bytes=60 * 1024 * 1024
        ),
        cost_estimate=pl.CostEstimate(flops=1800000000, bytes_accessed=14400000, transcendentals=100000),
    )(queries, cache_pool, page_table.T, lengths, residual, w_uv, w_out, norm_gain, w_gate.T, w_down)
    return pl.pallas_call(
        keep,
        out_shape=(jax.ShapeDtypeStruct((8, D), BF), jax.ShapeDtypeStruct((8, D), BF)),
        in_specs=[vmem, vmem],
        out_specs=(vmem, vmem),
    )(pltpu.with_memory_space_constraint(att, pltpu.VMEM), pltpu.with_memory_space_constraint(ffn, pltpu.VMEM))


def solution(mesh):
    return jax.shard_map(
        body,
        mesh=mesh,
        in_specs=(
            P(("grp", "rank"), None, None),
            P(("grp", "rank"), None, None),
            P(("grp", "rank"), None),
            P(("grp", "rank")),
            P(("grp", "rank"), None),
            P("rank", None, None),
            P("rank", None),
            P(),
            P(None, "rank"),
            P("rank", None),
        ),
        out_specs=(P(("grp", "rank"), None), P(("grp", "rank"), None)),
        check_vma=False,
    )
```

```python
import jax
import jax.numpy as jnp
from jax import lax
from jax.experimental import pallas as pl
from jax.experimental.pallas import tpu as pltpu
from jax.sharding import PartitionSpec as P

SCALE = 0.07216878364870322
LAT = 512
KW = 576
D = 3584
HALF = 1792
CH = 896
FFL = 576
Z = 8
NB = 2
BF = jnp.bfloat16
F32 = jnp.float32
NT = (((1,), (1,)), ((), ()))
MESH = pl.DeviceIdType.MESH
FAR = (4, 3, 5, 2, 6, 1, 7)


def kernel(
    q_h, pool_h, pt_h, ln_h, res_h, wuv_h, wout_h, gain_h, wg_h, wd_h,
    att_o, ffn_o,
    pt, ln, qv, poolv, resv, wuvv, woutv, gain1, gain2, gainv, wgv, wdv,
    ctxa, ctxb, rctx, lhs, vals,
    part, rsb, rrb, gown, xin, sq, pre, hid, res_s, res_r, att, fin, outx_r,
    lsem, a2a_s, a2a_r, w_ss, w_rs, v_ss, v_rs, rg_ss, rg_rs, ag_ss, ag_rs, h_ss, h_rs, ex_ss, ex_rs,
):
    me = lax.axis_index("rank")
    z = lax.div(me, 2)
    c = lax.rem(me, 2)
    sib = me + 1 - 2 * c
    other = {"rank": sib}
    odd = lax.rem(z, 2)
    two = 2 + 4 * odd

    def chip(j):
        return lax.rem(z + j, Z)

    own_col = pl.multiple_of(c * HALF, 128)
    oth_col = pl.multiple_of((1 - c) * HALF, 128)

    barrier = pltpu.get_barrier_semaphore()
    for k in (8, 9, 7, 6, 10, 5, 11, 4, 12, 3, 13, 2, 14, 1, 15):
        pl.semaphore_signal(barrier, inc=1, device_id={"rank": lax.rem(me + k, 16)}, device_id_type=MESH)

    copies = []
    sends = []

    def load(src, dst):
        cp = pltpu.make_async_copy(src, dst, lsem.at[len(copies)])
        copies.append(cp)
        cp.start()
        return cp

    l_pt = load(pt_h, pt)
    l_ln = load(ln_h, ln)
    l_q = [load(q_h.at[pl.ds(4 * i, 4)], qv.at[pl.ds(4 * i, 4)]) for i in range(NB)]
    l_pool = load(pool_h, poolv)
    l_res = load(res_h, resv)
    l_gain = load(gain_h, gain1)
    l_wuv = load(wuv_h, wuvv)
    l_wout = load(wout_h.at[:, pl.ds(own_col, HALF)], woutv.at[0])
    l_wg = load(wg_h.at[:, pl.ds(own_col, HALF)], wgv.at[0])
    l_wd = load(wd_h.at[:, pl.ds(own_col, HALF)], wdv.at[0])

    def remote(src, dst, ss, rs, dev):
        cp = pltpu.make_async_remote_copy(
            src_ref=src, dst_ref=dst, send_sem=ss, recv_sem=rs, device_id=dev, device_id_type=MESH
        )
        cp.start()
        sends.append(cp)

    def flush(keep):
        old = len(sends) - keep
        for cp in sends[:old]:
            cp.wait_send()
        del sends[:old]

    def arrived(dst, rs):
        pltpu.make_async_copy(dst, dst, rs).wait()

    ri = lax.broadcasted_iota(jnp.int32, (256, 256), 0)
    ci = lax.broadcasted_iota(jnp.int32, (256, 256), 1)
    to_rank = (ci == ((ri >> 2) & 3) * 64 + (ri >> 4) * 4 + (ri & 3)).astype(F32).astype(BF)
    to_head = (ci == (ri & 63) * 4 + (ri >> 6)).astype(F32).astype(BF)
    col = lax.broadcasted_iota(jnp.int32, (64, 128), 1)

    def attend(i):
        for r in range(4):
            b = 4 * i + r
            key = jnp.concatenate([poolv[pt[0, b]], poolv[pt[1, b]]], axis=0)
            s = lax.dot_general(qv[b], key, NT, preferred_element_type=F32) * SCALE
            s = jnp.where(col < ln[b], s, F32(-1e30))
            p = jnp.exp(s - jnp.max(s, axis=-1, keepdims=True))
            w = (p / jnp.sum(p, axis=-1, keepdims=True)).astype(BF)
            ctxa[i, pl.ds(r * 64, 64), :] = jnp.dot(w, key[:, :LAT], preferred_element_type=F32).astype(BF)
        ctxb[i] = jnp.dot(to_rank, ctxa[i], preferred_element_type=F32).astype(BF)

    def send_contexts(i):
        def block(rank):
            return pl.ds(pl.multiple_of(rank * 16, 16), 16)

        for j in FAR:
            for k in (0, 1):
                dst = chip(j) * 2 + k
                remote(
                    ctxb.at[i, block(dst), :], rctx.at[i, 8 - j, c], a2a_s.at[i, j, k], a2a_r.at[i, 8 - j, c], {"rank": dst}
                )
        remote(ctxb.at[i, block(sib), :], rctx.at[i, 0, c], a2a_s.at[i, 0, 0], a2a_r.at[i, 0, c], other)
        rctx[i, 0, c] = ctxb[i, block(me), :]

    def project(i):
        arrived(rctx.at[i, 0, 1 - c], a2a_r.at[i, 0, 1 - c])
        for j in FAR:
            for k in (0, 1):
                arrived(rctx.at[i, j, k], a2a_r.at[i, j, k])
        lhs[i] = jnp.dot(to_head, rctx[i].reshape(256, LAT), preferred_element_type=F32).astype(BF)
        for h in range(4):
            v = jnp.dot(lhs[i, pl.ds(h * 64, 64), :], wuvv[h], preferred_element_type=F32)
            vals[i, 0, :, pl.ds(h * 128, 128)] = v.astype(BF)
        remote(vals.at[i, 0], vals.at[i, 1], v_ss.at[i], v_rs.at[i], other)

    def multiply(t, i, left, weights, ready):
        for k in (0, 1):
            part[t, i, k] = jnp.dot(left[i, 0], weights[0, :, pl.ds(k * CH, CH)], preferred_element_type=F32)
        if ready:
            arrived(left.at[i, 1], v_rs.at[i])
        for k in (0, 1):
            o = jnp.dot(left[i, 1], weights[1, :, pl.ds(k * CH, CH)], preferred_element_type=F32)
            part[t, i, k] = part[t, i, k] + o

    def scatter_send(t, i, j, slot, dst, extra):
        rows = pl.ds(8 * j, 8)
        acc = jnp.concatenate([part[t, i, 0, rows, :], part[t, i, 1, rows, :]], axis=0)
        for e in extra:
            acc = acc + e
        rsb[t, i, j] = acc.astype(BF)
        remote(
            rsb.at[t, i, j], rrb.at[t, i, slot], rg_ss.at[t, i, j], rg_rs.at[t, i, slot], {"rank": dst * 2 + c}
        )

    def relayed(t, i):
        return t == 0 and i == 1

    def scatter_start(t, i):
        if not relayed(t, i):
            for j in FAR:
                scatter_send(t, i, j, 8 - j, chip(j), ())
        else:
            scatter_send(t, i, 4, 4, chip(two), ())
            scatter_send(t, i, 3, 3, chip(1), ())
            scatter_send(t, i, 5, 5, chip(7), ())
            scatter_send(t, i, 1, 7, chip(1), ())
            scatter_send(t, i, 7, 1, chip(7), ())

    def scatter_mid(t, i):
        arrived(rrb.at[t, i, 4], rg_rs.at[t, i, 4])
        far = rrb[t, i, 4].astype(F32)
        none = jnp.zeros_like(far)
        arrived(rrb.at[t, i, 3], rg_rs.at[t, i, 3])
        scatter_send(t, i, 2, 6, chip(2), (rrb[t, i, 3].astype(F32), jnp.where(odd == 0, far, none)))
        arrived(rrb.at[t, i, 5], rg_rs.at[t, i, 5])
        scatter_send(t, i, 6, 2, chip(6), (rrb[t, i, 5].astype(F32), jnp.where(odd == 0, none, far)))

    def scatter_end(t, i):
        acc = jnp.concatenate([part[t, i, 0, pl.ds(0, 8), :], part[t, i, 1, pl.ds(0, 8), :]], axis=0)
        for j in (1, 7, 2, 6) if relayed(t, i) else FAR:
            arrived(rrb.at[t, i, j], rg_rs.at[t, i, j])
            acc = acc + rrb[t, i, j].astype(F32)
        return acc

    def prepare(i, src, slot):
        rows = pl.ds(slot * 8, 8)
        v = src.astype(F32)
        tot = jnp.zeros((8, 128), F32)
        for k in (0, 1):
            u = v[8 * k : 8 * k + 8]
            xin[i, rows, pl.ds(k * CH, CH)] = u * gainv[:, pl.ds(k * CH, CH)]
            u = u * u
            for n in range(CH // 128):
                tot = tot + u[:, n * 128 : (n + 1) * 128]
        sq[i, 0, rows, :] = tot

    def gather_send(i, src, slot, dst):
        remote(gown.at[i, src], gown.at[i, slot], ag_ss.at[i, slot], ag_rs.at[i, slot], {"rank": dst * 2 + c})

    def gather_start(i, attn):
        res = jnp.concatenate(
            [res_r[c2, 4 * i : 4 * i + 4, k * CH : (k + 1) * CH] for k in (0, 1) for c2 in (0, 1)], axis=0
        )
        a = (attn + res).astype(BF)
        gown[i, 0] = a
        for j in FAR:
            gather_send(i, 0, 8 - j, chip(j))
        att[0, i] = a.astype(F32)
        remote(att.at[0, i], outx_r.at[0, i], ex_ss.at[1, i], ex_rs.at[1, i], other)
        prepare(i, a, 0)

    def gather_end(i):
        for j in FAR:
            arrived(gown.at[i, j], ag_rs.at[i, j])
            prepare(i, gown[i, j], j)
        remote(sq.at[i, 0], sq.at[i, 1], h_ss.at[i, 2], h_rs.at[i, 2], other)
        x = xin[i].astype(BF)
        for u in (1, 0):
            pre[i, 0, u] = lax.dot_general(x, wgv[u], NT, preferred_element_type=F32).astype(BF)
            remote(pre.at[i, 0, u], pre.at[i, 1, 1 - u], h_ss.at[i, u], h_rs.at[i, 1 - u], other)

    def activate(i):
        arrived(sq.at[i, 1], h_rs.at[i, 2])
        ms = jnp.sum(sq[i, 0] + sq[i, 1], axis=-1, keepdims=True) * F32(1.0 / D)
        inv = lax.rsqrt(ms + F32(1e-6))
        for u in (0, 1):
            arrived(pre.at[i, 1, u], h_rs.at[i, u])
            g = (pre[i, 0, u].astype(F32) + pre[i, 1, u].astype(F32)) * inv
            hid[i, u] = (g / (1.0 + jnp.exp(-g))).astype(BF)

    def push(src, dst, n):
        remote(src.at[:, pl.ds(oth_col, HALF)], dst.at[1], w_ss.at[n], w_rs.at[n], other)

    l_pt.wait()
    l_ln.wait()
    l_pool.wait()
    l_q[0].wait()
    attend(0)
    pl.semaphore_wait(barrier, 15)
    push(wout_h, woutv, 0)
    push(wg_h, wgv, 1)
    push(wd_h, wdv, 2)
    send_contexts(0)
    l_q[1].wait()
    attend(1)
    send_contexts(1)

    l_res.wait()
    res_r[c] = resv[:, pl.ds(own_col, HALF)].astype(F32)
    res_s[...] = resv[:, pl.ds(oth_col, HALF)].astype(F32)
    remote(res_s, res_r.at[c], ex_ss.at[0, 0], ex_rs.at[0, 0], other)
    l_gain.wait()
    gain2[...] = gain1[...].reshape(1, D)
    gainv[...] = gain2[:, pl.ds(own_col, HALF)]

    l_wuv.wait()
    l_wout.wait()
    arrived(woutv.at[1], w_rs.at[0])

    def finish(i):
        fin[i] = (att[0, i] + scatter_end(1, i)).astype(BF).astype(F32)
        remote(fin.at[i], outx_r.at[1, i], ex_ss.at[2, i], ex_rs.at[2, i], other)

    project(0)
    multiply(0, 0, vals, woutv, True)
    scatter_start(0, 0)
    project(1)
    multiply(0, 1, vals, woutv, True)
    scatter_start(0, 1)
    arrived(res_r.at[1 - c], ex_rs.at[0, 0])
    gather_start(0, scatter_end(0, 0))
    scatter_mid(0, 1)
    gather_start(1, scatter_end(0, 1))
    l_wg.wait()
    arrived(wgv.at[1], w_rs.at[1])
    l_wd.wait()
    arrived(wdv.at[1], w_rs.at[2])
    flush(16)
    gather_end(0)
    activate(0)
    multiply(1, 0, hid, wdv, False)
    scatter_start(1, 0)
    gather_end(1)
    activate(1)
    multiply(1, 1, hid, wdv, False)
    scatter_start(1, 1)
    flush(8)
    finish(0)
    finish(1)

    def rows_of(blocks, k):
        parts = []
        for i in range(NB):
            v = blocks[i]
            parts.append(jnp.where(c == 0, v[8 * k : 8 * k + 4], v[8 * k + 4 : 8 * k + 8]))
        return jnp.concatenate(parts, axis=0).astype(BF)

    for k in (0, 1):
        att_o[:, pl.ds(pl.multiple_of(own_col + k * CH, 128), CH)] = rows_of([att[0, i] for i in range(NB)], k)
        ffn_o[:, pl.ds(pl.multiple_of(own_col + k * CH, 128), CH)] = rows_of([fin[i] for i in range(NB)], k)
    for t, o in ((0, att_o), (1, ffn_o)):
        for i in range(NB):
            arrived(outx_r.at[t, i], ex_rs.at[t + 1, i])
        for k in (0, 1):
            o[:, pl.ds(pl.multiple_of(oth_col + k * CH, 128), CH)] = rows_of([outx_r[t, i] for i in range(NB)], k)
    flush(0)


def keep(a, b, att_o, ffn_o):
    att_o[...] = a[...]
    ffn_o[...] = b[...]


def body(queries, cache_pool, page_table, lengths, residual, w_uv, w_out, norm_gain, w_gate, w_down):
    anyspec = pl.BlockSpec(memory_space=pl.ANY)
    vmem = pl.BlockSpec(memory_space=pltpu.VMEM)
    V = pltpu.VMEM
    DMA = pltpu.SemaphoreType.DMA
    att, ffn = pl.pallas_call(
        kernel,
        out_shape=(V((8, D), BF), V((8, D), BF)),
        in_specs=[anyspec, anyspec, anyspec, anyspec] + [anyspec] * 6,
        out_specs=(vmem, vmem),
        scratch_shapes=[
            pltpu.SMEM((2, 8), jnp.int32), pltpu.SMEM((8,), jnp.int32), V((8, 64, KW), BF), V((16, 64, KW), BF), V((8, D), BF), V((4, LAT, 128), BF),
            V((2, 512, HALF), BF), V((D,), F32), V((1, D), F32), V((1, HALF), F32), V((2, FFL, HALF), BF), V((2, FFL, HALF), BF),
            V((NB, 256, LAT), BF), V((NB, 256, LAT), BF), V((NB, Z, 2, 16, LAT), BF), V((NB, 256, LAT), BF), V((NB, 2, 64, 512), BF),
            V((2, NB, 2, 64, CH), F32), V((2, NB, Z, 16, CH), BF), V((2, NB, Z, 16, CH), BF),
            V((NB, Z, 16, CH), BF), V((NB, 64, HALF), F32), V((NB, 2, 64, 128), F32), V((NB, 2, 2, 64, FFL), BF), V((NB, 2, 64, FFL), BF),
            V((8, HALF), F32), V((2, 8, HALF), F32), V((1, NB, 16, CH), F32), V((NB, 16, CH), F32), V((2, NB, 16, CH), F32),
            DMA((16,)), DMA((NB, Z, 2)), DMA((NB, Z, 2)), DMA((3,)), DMA((3,)), DMA((NB,)), DMA((NB,)), DMA((2, NB, Z)), DMA((2, NB, Z)),
            DMA((NB, Z)), DMA((NB, Z)), DMA((NB, 3)), DMA((NB, 3)), DMA((3, NB)), DMA((3, NB)),
        ],
        compiler_params=pltpu.CompilerParams(
            collective_id=0, has_side_effects=True, vmem_limit_bytes=60 * 1024 * 1024
        ),
        cost_estimate=pl.CostEstimate(flops=1800000000, bytes_accessed=14400000, transcendentals=100000),
    )(queries, cache_pool, page_table.T, lengths, residual, w_uv, w_out, norm_gain, w_gate.T, w_down)
    return pl.pallas_call(
        keep,
        out_shape=(jax.ShapeDtypeStruct((8, D), BF), jax.ShapeDtypeStruct((8, D), BF)),
        in_specs=[vmem, vmem],
        out_specs=(vmem, vmem),
    )(pltpu.with_memory_space_constraint(att, pltpu.VMEM), pltpu.with_memory_space_constraint(ffn, pltpu.VMEM))


def solution(mesh):
    return jax.shard_map(
        body,
        mesh=mesh,
        in_specs=(
            P(("grp", "rank"), None, None),
            P(("grp", "rank"), None, None),
            P(("grp", "rank"), None),
            P(("grp", "rank")),
            P(("grp", "rank"), None),
            P("rank", None, None),
            P("rank", None),
            P(),
            P(None, "rank"),
            P("rank", None),
        ),
        out_specs=(P(("grp", "rank"), None), P(("grp", "rank"), None)),
        check_vma=False,
    )
```

```python
import jax
import jax.numpy as jnp
from jax import lax
from jax.experimental import pallas as pl
from jax.experimental.pallas import tpu as pltpu
from jax.sharding import PartitionSpec as P

SCALE = 0.07216878364870322
LAT = 512
KW = 576
D = 3584
HALF = 1792
CH = 896
FFL = 576
Z = 8
NB = 2
BF = jnp.bfloat16
F32 = jnp.float32
NT = (((1,), (1,)), ((), ()))
MESH = pl.DeviceIdType.MESH
FAR = (4, 3, 5, 2, 6, 1, 7)


def kernel(
    q_h, pool_h, pt_h, ln_h, res_h, wuv_h, wout_h, gain_h, wg_h, wd_h,
    att_o, ffn_o,
    pt, ln, qv, poolv, resv, wuvv, woutv, gain1, gain2, gainv, wgv, wdv,
    ctxa, ctxb, rctx, lhs, vals,
    part, rsb, rrb, gown, xin, sq, pre, hid, res_s, res_r, att, fin, outx_r,
    lsem, a2a_s, a2a_r, w_ss, w_rs, v_ss, v_rs, rg_ss, rg_rs, ag_ss, ag_rs, h_ss, h_rs, ex_ss, ex_rs,
):
    me = lax.axis_index("rank")
    z = lax.div(me, 2)
    c = lax.rem(me, 2)
    sib = me + 1 - 2 * c
    other = {"rank": sib}
    odd = lax.rem(z, 2)
    two = 2 + 4 * odd

    def chip(j):
        return lax.rem(z + j, Z)

    own_col = pl.multiple_of(c * HALF, 128)
    oth_col = pl.multiple_of((1 - c) * HALF, 128)

    barrier = pltpu.get_barrier_semaphore()
    for k in (8, 9, 7, 6, 10, 5, 11, 4, 12, 3, 13, 2, 14, 1, 15):
        pl.semaphore_signal(barrier, inc=1, device_id={"rank": lax.rem(me + k, 16)}, device_id_type=MESH)

    copies = []
    sends = []

    def load(src, dst):
        cp = pltpu.make_async_copy(src, dst, lsem.at[len(copies)])
        copies.append(cp)
        cp.start()
        return cp

    l_pt = load(pt_h, pt)
    l_ln = load(ln_h, ln)
    l_q = [load(q_h.at[pl.ds(4 * i, 4)], qv.at[pl.ds(4 * i, 4)]) for i in range(NB)]
    l_pool = load(pool_h, poolv)
    l_res = load(res_h, resv)
    l_gain = load(gain_h, gain1)
    l_wuv = load(wuv_h, wuvv)
    l_wout = load(wout_h.at[:, pl.ds(own_col, HALF)], woutv.at[0])
    l_wg = load(wg_h.at[:, pl.ds(own_col, HALF)], wgv.at[0])
    l_wd = load(wd_h.at[:, pl.ds(own_col, HALF)], wdv.at[0])

    def remote(src, dst, ss, rs, dev):
        cp = pltpu.make_async_remote_copy(
            src_ref=src, dst_ref=dst, send_sem=ss, recv_sem=rs, device_id=dev, device_id_type=MESH
        )
        cp.start()
        sends.append(cp)

    def flush(keep):
        old = len(sends) - keep
        for cp in sends[:old]:
            cp.wait_send()
        del sends[:old]

    def arrived(dst, rs):
        pltpu.make_async_copy(dst, dst, rs).wait()

    ri = lax.broadcasted_iota(jnp.int32, (256, 256), 0)
    ci = lax.broadcasted_iota(jnp.int32, (256, 256), 1)
    to_rank = (ci == ((ri >> 2) & 3) * 64 + (ri >> 4) * 4 + (ri & 3)).astype(F32).astype(BF)
    to_head = (ci == (ri & 63) * 4 + (ri >> 6)).astype(F32).astype(BF)
    col = lax.broadcasted_iota(jnp.int32, (64, 128), 1)

    def attend(i):
        for r in range(4):
            b = 4 * i + r
            key = jnp.concatenate([poolv[pt[0, b]], poolv[pt[1, b]]], axis=0)
            s = lax.dot_general(qv[b], key, NT, preferred_element_type=F32) * SCALE
            s = jnp.where(col < ln[b], s, F32(-1e30))
            p = jnp.exp(s - jnp.max(s, axis=-1, keepdims=True))
            w = (p / jnp.sum(p, axis=-1, keepdims=True)).astype(BF)
            ctxa[i, pl.ds(r * 64, 64), :] = jnp.dot(w, key[:, :LAT], preferred_element_type=F32).astype(BF)
        ctxb[i] = jnp.dot(to_rank, ctxa[i], preferred_element_type=F32).astype(BF)

    def send_contexts(i):
        def block(rank):
            return pl.ds(pl.multiple_of(rank * 16, 16), 16)

        for j in FAR:
            for k in (0, 1):
                dst = chip(j) * 2 + k
                remote(
                    ctxb.at[i, block(dst), :], rctx.at[i, 8 - j, c], a2a_s.at[i, j, k], a2a_r.at[i, 8 - j, c], {"rank": dst}
                )
        remote(ctxb.at[i, block(sib), :], rctx.at[i, 0, c], a2a_s.at[i, 0, 0], a2a_r.at[i, 0, c], other)
        rctx[i, 0, c] = ctxb[i, block(me), :]

    def project(i):
        arrived(rctx.at[i, 0, 1 - c], a2a_r.at[i, 0, 1 - c])
        for j in FAR:
            for k in (0, 1):
                arrived(rctx.at[i, j, k], a2a_r.at[i, j, k])
        lhs[i] = jnp.dot(to_head, rctx[i].reshape(256, LAT), preferred_element_type=F32).astype(BF)
        for h in range(4):
            v = jnp.dot(lhs[i, pl.ds(h * 64, 64), :], wuvv[h], preferred_element_type=F32)
            vals[i, 0, :, pl.ds(h * 128, 128)] = v.astype(BF)
        remote(vals.at[i, 0], vals.at[i, 1], v_ss.at[i], v_rs.at[i], other)

    def multiply(t, i, left, weights, ready):
        for k in (0, 1):
            part[t, i, k] = jnp.dot(left[i, 0], weights[0, :, pl.ds(k * CH, CH)], preferred_element_type=F32)
        if ready:
            arrived(left.at[i, 1], v_rs.at[i])
        for k in (0, 1):
            o = jnp.dot(left[i, 1], weights[1, :, pl.ds(k * CH, CH)], preferred_element_type=F32)
            part[t, i, k] = part[t, i, k] + o

    def scatter_send(t, i, j, slot, dst, extra):
        rows = pl.ds(8 * j, 8)
        acc = jnp.concatenate([part[t, i, 0, rows, :], part[t, i, 1, rows, :]], axis=0)
        for e in extra:
            acc = acc + e
        rsb[t, i, j] = acc.astype(BF)
        remote(
            rsb.at[t, i, j], rrb.at[t, i, slot], rg_ss.at[t, i, j], rg_rs.at[t, i, slot], {"rank": dst * 2 + c}
        )

    def relayed(t, i):
        return t == 0 and i == 1

    def scatter_start(t, i):
        if not relayed(t, i):
            for j in FAR:
                scatter_send(t, i, j, 8 - j, chip(j), ())
        else:
            scatter_send(t, i, 4, 4, chip(two), ())
            scatter_send(t, i, 3, 3, chip(1), ())
            scatter_send(t, i, 5, 5, chip(7), ())
            scatter_send(t, i, 1, 7, chip(1), ())
            scatter_send(t, i, 7, 1, chip(7), ())

    def scatter_mid(t, i):
        arrived(rrb.at[t, i, 4], rg_rs.at[t, i, 4])
        far = rrb[t, i, 4].astype(F32)
        none = jnp.zeros_like(far)
        arrived(rrb.at[t, i, 3], rg_rs.at[t, i, 3])
        scatter_send(t, i, 2, 6, chip(2), (rrb[t, i, 3].astype(F32), jnp.where(odd == 0, far, none)))
        arrived(rrb.at[t, i, 5], rg_rs.at[t, i, 5])
        scatter_send(t, i, 6, 2, chip(6), (rrb[t, i, 5].astype(F32), jnp.where(odd == 0, none, far)))

    def scatter_end(t, i):
        acc = jnp.concatenate([part[t, i, 0, pl.ds(0, 8), :], part[t, i, 1, pl.ds(0, 8), :]], axis=0)
        for j in (1, 7, 2, 6) if relayed(t, i) else FAR:
            arrived(rrb.at[t, i, j], rg_rs.at[t, i, j])
            acc = acc + rrb[t, i, j].astype(F32)
        return acc

    def prepare(i, src, slot):
        rows = pl.ds(slot * 8, 8)
        v = src.astype(F32)
        tot = jnp.zeros((8, 128), F32)
        for k in (0, 1):
            u = v[8 * k : 8 * k + 8]
            xin[i, rows, pl.ds(k * CH, CH)] = u * gainv[:, pl.ds(k * CH, CH)]
            u = u * u
            for n in range(CH // 128):
                tot = tot + u[:, n * 128 : (n + 1) * 128]
        sq[i, 0, rows, :] = tot

    def gather_send(i, src, slot, dst):
        remote(gown.at[i, src], gown.at[i, slot], ag_ss.at[i, slot], ag_rs.at[i, slot], {"rank": dst * 2 + c})

    def gather_start(i, attn):
        res = jnp.concatenate(
            [res_r[c2, 4 * i : 4 * i + 4, k * CH : (k + 1) * CH] for k in (0, 1) for c2 in (0, 1)], axis=0
        )
        a = (attn + res).astype(BF)
        gown[i, 0] = a
        for j in FAR:
            gather_send(i, 0, 8 - j, chip(j))
        att[0, i] = a.astype(F32)
        remote(att.at[0, i], outx_r.at[0, i], ex_ss.at[1, i], ex_rs.at[1, i], other)
        prepare(i, a, 0)

    def gather_end(i):
        for j in FAR:
            arrived(gown.at[i, j], ag_rs.at[i, j])
            prepare(i, gown[i, j], j)
        remote(sq.at[i, 0], sq.at[i, 1], h_ss.at[i, 2], h_rs.at[i, 2], other)
        x = xin[i].astype(BF)
        for u in (1, 0):
            pre[i, 0, u] = lax.dot_general(x, wgv[u], NT, preferred_element_type=F32).astype(BF)
            remote(pre.at[i, 0, u], pre.at[i, 1, 1 - u], h_ss.at[i, u], h_rs.at[i, 1 - u], other)

    def activate(i):
        arrived(sq.at[i, 1], h_rs.at[i, 2])
        ms = jnp.sum(sq[i, 0] + sq[i, 1], axis=-1, keepdims=True) * F32(1.0 / D)
        inv = lax.rsqrt(ms + F32(1e-6))
        for u in (0, 1):
            arrived(pre.at[i, 1, u], h_rs.at[i, u])
            g = (pre[i, 0, u].astype(F32) + pre[i, 1, u].astype(F32)) * inv
            hid[i, u] = (g / (1.0 + jnp.exp(-g))).astype(BF)

    def push(src, dst, n):
        remote(src.at[:, pl.ds(oth_col, HALF)], dst.at[1], w_ss.at[n], w_rs.at[n], other)

    l_pt.wait()
    l_ln.wait()
    l_pool.wait()
    l_q[0].wait()
    attend(0)
    pl.semaphore_wait(barrier, 15)
    push(wout_h, woutv, 0)
    push(wg_h, wgv, 1)
    push(wd_h, wdv, 2)
    send_contexts(0)
    l_q[1].wait()
    attend(1)
    send_contexts(1)

    l_wuv.wait()
    l_wout.wait()
    arrived(woutv.at[1], w_rs.at[0])

    def finish(i):
        fin[i] = (att[0, i] + scatter_end(1, i)).astype(BF).astype(F32)
        remote(fin.at[i], outx_r.at[1, i], ex_ss.at[2, i], ex_rs.at[2, i], other)

    project(0)
    l_res.wait()
    res_r[c] = resv[:, pl.ds(own_col, HALF)].astype(F32)
    res_s[...] = resv[:, pl.ds(oth_col, HALF)].astype(F32)
    remote(res_s, res_r.at[c], ex_ss.at[0, 0], ex_rs.at[0, 0], other)
    l_gain.wait()
    gain2[...] = gain1[...].reshape(1, D)
    gainv[...] = gain2[:, pl.ds(own_col, HALF)]

    multiply(0, 0, vals, woutv, True)
    scatter_start(0, 0)
    project(1)
    multiply(0, 1, vals, woutv, True)
    scatter_start(0, 1)
    arrived(res_r.at[1 - c], ex_rs.at[0, 0])
    gather_start(0, scatter_end(0, 0))
    scatter_mid(0, 1)
    gather_start(1, scatter_end(0, 1))
    l_wg.wait()
    arrived(wgv.at[1], w_rs.at[1])
    l_wd.wait()
    arrived(wdv.at[1], w_rs.at[2])
    flush(16)
    gather_end(0)
    activate(0)
    multiply(1, 0, hid, wdv, False)
    scatter_start(1, 0)
    gather_end(1)
    activate(1)
    multiply(1, 1, hid, wdv, False)
    scatter_start(1, 1)
    flush(8)
    finish(0)
    finish(1)

    def rows_of(blocks, k):
        parts = []
        for i in range(NB):
            v = blocks[i]
            parts.append(jnp.where(c == 0, v[8 * k : 8 * k + 4], v[8 * k + 4 : 8 * k + 8]))
        return jnp.concatenate(parts, axis=0).astype(BF)

    for k in (0, 1):
        att_o[:, pl.ds(pl.multiple_of(own_col + k * CH, 128), CH)] = rows_of([att[0, i] for i in range(NB)], k)
        ffn_o[:, pl.ds(pl.multiple_of(own_col + k * CH, 128), CH)] = rows_of([fin[i] for i in range(NB)], k)
    for t, o in ((0, att_o), (1, ffn_o)):
        for i in range(NB):
            arrived(outx_r.at[t, i], ex_rs.at[t + 1, i])
        for k in (0, 1):
            o[:, pl.ds(pl.multiple_of(oth_col + k * CH, 128), CH)] = rows_of([outx_r[t, i] for i in range(NB)], k)
    flush(0)


def keep(a, b, att_o, ffn_o):
    att_o[...] = a[...]
    ffn_o[...] = b[...]


def body(queries, cache_pool, page_table, lengths, residual, w_uv, w_out, norm_gain, w_gate, w_down):
    anyspec = pl.BlockSpec(memory_space=pl.ANY)
    vmem = pl.BlockSpec(memory_space=pltpu.VMEM)
    V = pltpu.VMEM
    DMA = pltpu.SemaphoreType.DMA
    att, ffn = pl.pallas_call(
        kernel,
        out_shape=(V((8, D), BF), V((8, D), BF)),
        in_specs=[anyspec, anyspec, anyspec, anyspec] + [anyspec] * 6,
        out_specs=(vmem, vmem),
        scratch_shapes=[
            pltpu.SMEM((2, 8), jnp.int32), pltpu.SMEM((8,), jnp.int32), V((8, 64, KW), BF), V((16, 64, KW), BF), V((8, D), BF), V((4, LAT, 128), BF),
            V((2, 512, HALF), BF), V((D,), F32), V((1, D), F32), V((1, HALF), F32), V((2, FFL, HALF), BF), V((2, FFL, HALF), BF),
            V((NB, 256, LAT), BF), V((NB, 256, LAT), BF), V((NB, Z, 2, 16, LAT), BF), V((NB, 256, LAT), BF), V((NB, 2, 64, 512), BF),
            V((2, NB, 2, 64, CH), F32), V((2, NB, Z, 16, CH), BF), V((2, NB, Z, 16, CH), BF),
            V((NB, Z, 16, CH), BF), V((NB, 64, HALF), F32), V((NB, 2, 64, 128), F32), V((NB, 2, 2, 64, FFL), BF), V((NB, 2, 64, FFL), BF),
            V((8, HALF), F32), V((2, 8, HALF), F32), V((1, NB, 16, CH), F32), V((NB, 16, CH), F32), V((2, NB, 16, CH), F32),
            DMA((16,)), DMA((NB, Z, 2)), DMA((NB, Z, 2)), DMA((3,)), DMA((3,)), DMA((NB,)), DMA((NB,)), DMA((2, NB, Z)), DMA((2, NB, Z)),
            DMA((NB, Z)), DMA((NB, Z)), DMA((NB, 3)), DMA((NB, 3)), DMA((3, NB)), DMA((3, NB)),
        ],
        compiler_params=pltpu.CompilerParams(
            collective_id=0, has_side_effects=True, vmem_limit_bytes=60 * 1024 * 1024
        ),
        cost_estimate=pl.CostEstimate(flops=1800000000, bytes_accessed=14400000, transcendentals=100000),
    )(queries, cache_pool, page_table.T, lengths, residual, w_uv, w_out, norm_gain, w_gate.T, w_down)
    return pl.pallas_call(
        keep,
        out_shape=(jax.ShapeDtypeStruct((8, D), BF), jax.ShapeDtypeStruct((8, D), BF)),
        in_specs=[vmem, vmem],
        out_specs=(vmem, vmem),
    )(pltpu.with_memory_space_constraint(att, pltpu.VMEM), pltpu.with_memory_space_constraint(ffn, pltpu.VMEM))


def solution(mesh):
    return jax.shard_map(
        body,
        mesh=mesh,
        in_specs=(
            P(("grp", "rank"), None, None),
            P(("grp", "rank"), None, None),
            P(("grp", "rank"), None),
            P(("grp", "rank")),
            P(("grp", "rank"), None),
            P("rank", None, None),
            P("rank", None),
            P(),
            P(None, "rank"),
            P("rank", None),
        ),
        out_specs=(P(("grp", "rank"), None), P(("grp", "rank"), None)),
        check_vma=False,
    )
```
